128 devices in a mesh: ctx: 32 (over z, x, y_hi), head: 4 (over y_lo, core).
Axes of the slice: x: 4, y: 4 (y_hi: 2, y_lo: 2; y = y_hi * 2 + y_lo), z: 4, core: 2. Of those that a mesh axis runs over, the one named last changes fastest.
Arguments:
- probe_vectors: bfloat16 [1024, 8192], P('ctx', 'head'), may hold values from -160 to 160
- lookup_tensor: bfloat16 [32768, 1024], P('ctx', 'head'), may hold values from -4.5 to 4.5
- payload_tensor: bfloat16 [32768, 1024], P('ctx', 'head'), may hold values from -6 to 6
- sequence_locations: int32 [1024], replicated, may hold values from 0 to 32767, as said below
- attention_return_matrix: bfloat16 [8192, 8192], P('head', 'ctx'), may hold values from -0.0625 to 0.0625
- skip_stream_state: bfloat16 [1024, 8192], P('head', 'ctx'), may hold values from -4 to 4
- early_rescaling_factor: float32 [8192], P('ctx'), may hold values from 0.5 to 1.5
- lexicon_projection_matrix: bfloat16 [8192, 65536], P(None, ('ctx', 'head')), may hold values from -0.1875 to 0.1875
- calibrating_divisor: float32 [1024], replicated, may hold values from 0.02 to 1
- desired_tokens_list: int32 [1024], replicated, may hold values from 0 to 65535
Outputs:
- hidden: bfloat16 [1024, 8192], P('head', 'ctx')
- logprob: float32 [1024], replicated
The draws below stay inside these ranges and needn't reach their ends.
Inputs may be any that keep to these rules, and one draw needn't show every extreme that they name: `sequence_locations`: query i stands at a position from i * 32 to (i + 1) * 32 - 1; the last query stands at 32767.
All inputs are finite; a program needn't handle non-finite values.
Results may differ from the reference program's by a relative error of at most 0.0014.
The reference program's roundings to bfloat16 on the way count: a program that leaves them out, or rounds other values in their place, can miss the bound.
Values may be sent and summed in bfloat16 or wider, within the bound.
A program may use at most 192 MiB of HBM per device.

```python
import math
import jax
import jax.numpy as jnp
import numpy as np
from jax import lax

D = 8192
QUERY_HEAD_COUNT = 64
KEY_VALUE_HEADS = 8
HEAD_SIZE = 128
V = 65536
EXIT_QUERIES = 1024
CONTEXT_PER_PART = 1024
CONTEXT_TOTAL = 32768


def position_draw(key):
    span = CONTEXT_TOTAL // EXIT_QUERIES
    offsets = jax.random.randint(jax.random.fold_in(key, 3), (EXIT_QUERIES,), 0, span)
    row_ids = jnp.arange(EXIT_QUERIES, dtype=jnp.int32)
    offsets = jnp.where(row_ids == EXIT_QUERIES - 1, 0, offsets)
    return ((row_ids + 1) * span - 1 - offsets).astype(jnp.int32)


def attention_draw(key):
    base_offset = jax.random.fold_in(key, 11)
    query_vals = 2.5 * jax.random.normal(jax.random.fold_in(base_offset, 1), (EXIT_QUERIES, QUERY_HEAD_COUNT * HEAD_SIZE), jnp.float32)
    query_vals = jnp.clip(query_vals, -12.0, 12.0)
    key_entries = jax.random.normal(jax.random.fold_in(base_offset, 2), (CONTEXT_TOTAL, KEY_VALUE_HEADS * HEAD_SIZE), jnp.float32)
    key_entries = jnp.clip(key_entries, -4.5, 4.5)
    return (query_vals, key_entries)


def draw_sequence_locations(key, part):
    return position_draw(key)


def draw_probe_vectors(key, part):
    return attention_draw(key)[0].astype(jnp.bfloat16)


def draw_lookup_tensor(key, part):
    return attention_draw(key)[1].astype(jnp.bfloat16)


def draw_calibrating_divisor(key, part):
    base_offset = jax.random.fold_in(key, 23)
    spread = jax.random.uniform(base_offset, (EXIT_QUERIES,), jnp.float32)
    temps = 0.25 * 4.0 ** spread
    return temps


def place_ends(drawn, own_key, smallest, high):
    longest = drawn.shape.index(max(drawn.shape))
    spots = []
    for shift in (0, 1):
        where = [jax.random.randint(jax.random.fold_in(own_key, axis), (), 0, length) for axis, length in enumerate(drawn.shape)]
        where[longest] = (where[longest] + shift) % drawn.shape[longest]
        spots.append(tuple(where))
    return drawn.at[spots[0]].set(smallest).at[spots[1]].set(high)


def block_levels(stream_key, extent, cuts, least, largest):
    gain, own = 1.0, jax.random.fold_in(stream_key, 6)
    for axis_at, blocks in cuts:
        heights = jnp.exp(jax.random.uniform(jax.random.fold_in(own, axis_at), (blocks,), jnp.float32, least / len(cuts), largest / len(cuts)))
        gain = gain * jnp.repeat(heights, extent[axis_at] // blocks).reshape([-1 if axis == axis_at else 1 for axis in range(len(extent))])
    return gain


def rank_table(count, lean):
    portions = [(1 << 20) // math.isqrt(standing ** lean) + 1 for standing in range(1, count + 1)]
    width = 1 + sum(portions) // (1 << 30)
    return np.cumsum(np.array([max(1, weight // width) for weight in portions]))


def ranked(own_key, extent, amount, lean):
    grid = rank_table(amount, lean)
    pick = jax.random.randint(jax.random.fold_in(own_key, 1), extent, 0, int(grid[amount - 1]))
    standing = jnp.searchsorted(jnp.asarray(grid, jnp.int32), pick, side="right")
    return jax.random.permutation(jax.random.fold_in(own_key, 2), amount)[standing].astype(jnp.int32)


def noise(stream_key, dims, scale, reach, split=(), held_as=jnp.bfloat16):
    level = block_levels(stream_key, dims, split, -0.22, 0.18) if split else 1.0
    result = jax.random.normal(stream_key, dims, jnp.float32) * scale * level
    return jnp.minimum(jnp.maximum(result, -reach), reach).astype(held_as)


def setup_inputs(seed: int = 0) -> dict:
    streams_of = jax.random.split(jax.random.key(seed), 11)
    probe_vectors = draw_probe_vectors(jax.random.fold_in(streams_of[10], 71), 0)
    lookup_tensor = draw_lookup_tensor(jax.random.fold_in(streams_of[10], 71), 0)
    payload_tensor = noise(streams_of[2], (CONTEXT_TOTAL, KEY_VALUE_HEADS * HEAD_SIZE), 1.0, 6.0, ((0, 32), (1, 4)))
    sequence_locations = draw_sequence_locations(jax.random.fold_in(streams_of[10], 71), 0)
    attention_return_matrix = noise(streams_of[4], (QUERY_HEAD_COUNT * HEAD_SIZE, D), (QUERY_HEAD_COUNT * HEAD_SIZE) ** -0.5, 0.0625, ((0, 4), (1, 32)))
    skip_stream_state = noise(streams_of[5], (EXIT_QUERIES, D), 0.3, 4.0, ((0, 4), (1, 32)))
    early_rescaling_factor = jnp.clip(1.0 + 0.1 * jax.random.normal(streams_of[6], (D,), jnp.float32), 0.5, 1.5)
    lexicon_projection_matrix = noise(streams_of[7], (D, V), (D // 9) ** -0.5, 0.1875, ((1, 128),))
    calibrating_divisor = draw_calibrating_divisor(jax.random.fold_in(streams_of[10], 71), 0)
    desired_tokens_list = place_ends(ranked(streams_of[9], (EXIT_QUERIES,), V, 2), jax.random.fold_in(streams_of[9], 3), 0, V - 1).astype(jnp.int32)
    return {"probe_vectors": probe_vectors, "lookup_tensor": lookup_tensor, "payload_tensor": payload_tensor, "sequence_locations": sequence_locations, "attention_return_matrix": attention_return_matrix, "skip_stream_state": skip_stream_state, "early_rescaling_factor": early_rescaling_factor, "lexicon_projection_matrix": lexicon_projection_matrix, "calibrating_divisor": calibrating_divisor, "desired_tokens_list": desired_tokens_list}


neg_big = -1e+30
eps = 1e-05

def head_attention(inputs, sequence_locations):
    query_head, key_head, value_head = inputs
    group_size = query_head.shape[1]
    scale_factor = HEAD_SIZE ** (-0.5)
    number_blocks = key_head.shape[0]
    start = (jnp.full((EXIT_QUERIES, group_size), neg_big, jnp.float32), jnp.zeros((EXIT_QUERIES, group_size), jnp.float32), jnp.zeros((EXIT_QUERIES, group_size, HEAD_SIZE), jnp.float32))

    def one_block(carry, block_inputs):
        run_max, run_sum, run_acc = carry
        key_block, value_block, block_index = block_inputs
        key_pos = block_index * CONTEXT_PER_PART + jnp.arange(CONTEXT_PER_PART, dtype=jnp.int32)
        scores = jnp.einsum('qhd,kd->qhk', query_head, key_block.astype(jnp.float32), precision=lax.Precision.HIGHEST) * scale_factor
        visible = key_pos[None, None, :] <= sequence_locations[:, None, None]
        block_max = lax.optimization_barrier(jnp.max(jnp.where(visible, scores, neg_big), axis=-1))
        weights = jnp.where(visible, jnp.exp(scores - block_max[..., None]), 0.0)
        block_sum = lax.optimization_barrier(jnp.sum(weights, axis=-1))
        rounded = lax.optimization_barrier(weights.astype(jnp.bfloat16)).astype(jnp.float32)
        block_acc = jnp.einsum('qhk,kd->qhd', rounded, value_block.astype(jnp.float32), precision=lax.Precision.HIGHEST)
        new_max = jnp.maximum(run_max, block_max)
        old_scale = jnp.exp(run_max - new_max)
        new_scale = jnp.exp(block_max - new_max)
        next_sum = run_sum * old_scale + block_sum * new_scale
        next_acc = run_acc * old_scale[..., None] + block_acc * new_scale[..., None]
        return ((new_max, next_sum, next_acc), None)
    block_ids = jnp.arange(number_blocks, dtype=jnp.int32)
    final, unused = lax.scan(one_block, start, (key_head, value_head, block_ids))
    return final[2] / final[1][..., None]

def reference(probe_vectors, lookup_tensor, payload_tensor, sequence_locations, attention_return_matrix, skip_stream_state, early_rescaling_factor, lexicon_projection_matrix, calibrating_divisor, desired_tokens_list):
    group_size = QUERY_HEAD_COUNT // KEY_VALUE_HEADS
    number_blocks = CONTEXT_TOTAL // CONTEXT_PER_PART
    every_query = probe_vectors.astype(jnp.float32).reshape(EXIT_QUERIES, KEY_VALUE_HEADS, group_size, HEAD_SIZE).transpose(1, 0, 2, 3)
    every_key = lookup_tensor.reshape(number_blocks, CONTEXT_PER_PART, KEY_VALUE_HEADS, HEAD_SIZE).transpose(2, 0, 1, 3)
    every_value = payload_tensor.reshape(number_blocks, CONTEXT_PER_PART, KEY_VALUE_HEADS, HEAD_SIZE).transpose(2, 0, 1, 3)
    heads_out = lax.map(lambda inputs: head_attention(inputs, sequence_locations), (every_query, every_key, every_value))
    attn = heads_out.transpose(1, 0, 2, 3).reshape(EXIT_QUERIES, QUERY_HEAD_COUNT * HEAD_SIZE).astype(jnp.bfloat16)
    mixed = jnp.dot(attn, attention_return_matrix, preferred_element_type=jnp.float32)
    hidden = (skip_stream_state.astype(jnp.float32) + mixed).astype(jnp.bfloat16)
    wide = hidden.astype(jnp.float32)
    mean_sq = lax.optimization_barrier(jnp.sum(wide * wide, axis=1)) / D
    normed = (wide * lax.rsqrt(mean_sq + eps)[:, None] * early_rescaling_factor[None, :]).astype(jnp.bfloat16)
    early_class_energies = jnp.dot(normed, lexicon_projection_matrix, preferred_element_type=jnp.float32)
    tempered_affinities = early_class_energies / calibrating_divisor[:, None]
    peak = lax.optimization_barrier(jnp.max(tempered_affinities, axis=1))
    total = lax.optimization_barrier(jnp.sum(jnp.exp(tempered_affinities - peak[:, None]), axis=1))
    picked = jnp.take_along_axis(tempered_affinities, desired_tokens_list[:, None].astype(jnp.int32), axis=1)[:, 0]
    logprob = picked - peak - jnp.log(total)
    return (hidden, logprob)
```

```python
import jax
import jax.numpy as jnp
from jax import lax
from jax.experimental import pallas as pl
from jax.experimental.pallas import tpu as pltpu
from jax.sharding import Mesh
from jax.sharding import PartitionSpec as P

D = 8192
EPS = 1e-05
LOW = -1e30
LOG2E = 1.4426950408889634
EXP2_SCALE = 128 ** (-0.5) * LOG2E
CTX = ("ctx_0", "ctx_1", "ctx_2")
HEAD = ("head_0", "head_1")
CTX_HEAD = CTX + HEAD
F32 = jnp.float32
BF16 = jnp.bfloat16
MESH = pl.DeviceIdType.MESH


def at_z(p):
    return {"ctx_0": p}


def at_x(p):
    return {"ctx_1": p}


def at_y(p):
    return {"ctx_2": lax.div(p, 2), "head_0": lax.rem(p, 2)}


def at_core(p):
    return {"head_1": p}


def around(p, d):
    return lax.rem(p + d, 4)


def remote(src, dst, ssem, rsem, dev):
    return pltpu.make_async_remote_copy(
        src_ref=src, dst_ref=dst, send_sem=ssem, recv_sem=rsem, device_id=dev, device_id_type=MESH
    )


def greet(dev):
    pl.semaphore_signal(pltpu.get_barrier_semaphore(), inc=1, device_id=dev, device_id_type=MESH)


def attend_kernel(
    q_hbm, k_hbm, v_hbm, loc_ref, out_ref,
    qbuf, kbuf, vbuf, m_s, l_s, acc, stat, racc, rstat,
    q_ss, q_rs, kv_ls, kv_ss, kv_rs, o_ss, o_rs,
):
    z, x, yh = lax.axis_index("ctx_0"), lax.axis_index("ctx_1"), lax.axis_index("ctx_2")
    k_me = 2 * x + yh
    plus, minus, opp = around(z, 1), around(z, 3), around(z, 2)
    diagonal = x == z

    greet(at_z(plus))
    greet(at_z(minus))
    for i in range(8):
        @pl.when(i != k_me)
        def _():
            greet({"ctx_1": i // 2, "ctx_2": i % 2})
    for i in range(8):
        src_z, src_y = i // 2, i % 2
        @pl.when(jnp.logical_not(diagonal & (src_z == z) & (src_y == yh)))
        def _():
            greet({"ctx_0": src_z, "ctx_1": z, "ctx_2": src_y})
    pl.semaphore_wait(pltpu.get_barrier_semaphore(), 2 + 7 + jnp.where(diagonal, 7, 8))

    slot_me = 2 * z + yh
    for i in range(8):
        to_self = diagonal & (i == k_me)
        @pl.when(jnp.logical_not(to_self))
        def _():
            remote(q_hbm, qbuf.at[slot_me], q_ss.at[i], q_rs.at[slot_me],
                   {"ctx_0": x, "ctx_1": i // 2, "ctx_2": i % 2}).start()
        @pl.when(to_self)
        def _():
            pltpu.make_async_copy(q_hbm, qbuf.at[slot_me], q_rs.at[slot_me]).start()

    own_k = pltpu.make_async_copy(k_hbm, kbuf.at[z], kv_ls.at[0])
    own_v = pltpu.make_async_copy(v_hbm, vbuf.at[z], kv_ls.at[1])
    own_k.start()
    own_v.start()
    k_plus = remote(k_hbm, kbuf.at[z], kv_ss.at[0], kv_rs.at[0], at_z(plus))
    v_minus = remote(v_hbm, vbuf.at[z], kv_ss.at[1], kv_rs.at[1], at_z(minus))
    v_plus = remote(v_hbm, vbuf.at[z], kv_ss.at[2], kv_rs.at[2], at_z(plus))
    k_minus = remote(k_hbm, kbuf.at[z], kv_ss.at[3], kv_rs.at[3], at_z(minus))
    k_plus.start()
    v_minus.start()
    v_plus.start()
    k_minus.start()
    k_on = remote(kbuf.at[minus], kbuf.at[minus], kv_ss.at[4], kv_rs.at[4], at_z(plus))
    v_on = remote(vbuf.at[plus], vbuf.at[plus], kv_ss.at[5], kv_rs.at[5], at_z(minus))

    m_s[...] = jnp.full(m_s.shape, LOW, F32)
    l_s[...] = jnp.zeros(l_s.shape, F32)
    acc[...] = jnp.zeros(acc.shape, F32)

    own_k.wait()
    own_v.wait()
    for i in range(8):
        remote(qbuf.at[i], qbuf.at[i], q_ss.at[0], q_rs.at[i], at_z(plus)).wait_recv()

    def tile(s, zo, g, masked):
        q = jnp.concatenate(
            [qbuf[s, :, (g * 8 + j) * 128 : (g * 8 + j + 1) * 128] for j in range(8)], axis=0
        )
        raw = lax.dot_general(
            q, kbuf[zo, :, g * 128 : (g + 1) * 128], (((1,), (1,)), ((), ())),
            preferred_element_type=F32,
        )
        if masked:
            base = 8 * zo + k_me
            first = pl.multiple_of(base * 32, 32)
            loc = loc_ref[pl.ds(first, 32), :] - base * 1024
            loc = jnp.concatenate([loc] * 8, axis=0)
            pos = lax.broadcasted_iota(jnp.int32, raw.shape, 1)
            raw = jnp.where(pos <= loc, raw, LOW)
        top = jnp.max(raw, axis=1, keepdims=True)
        w = jnp.exp2((raw - top) * EXP2_SCALE)
        total = jnp.sum(w, axis=1, keepdims=True)
        part = jnp.dot(
            w.astype(BF16), vbuf[zo, :, g * 128 : (g + 1) * 128], preferred_element_type=F32
        )
        m_old = m_s[s, g]
        m_new = jnp.maximum(m_old, top)
        a = jnp.exp2((m_old - m_new) * EXP2_SCALE)
        b = jnp.exp2((top - m_new) * EXP2_SCALE)
        m_s[s, g] = m_new
        l_s[s, g] = l_s[s, g] * a + total * b
        acc[s, g] = acc[s, g] * a + part * b

    def work(s, zo):
        chunk = 8 * lax.div(s, 2) + 2 * z + lax.rem(s, 2)
        block = 8 * zo + k_me

        @pl.when(chunk > block)
        def _():
            for g in range(2):
                tile(s, zo, g, False)

        @pl.when(chunk == block)
        def _():
            for g in range(2):
                tile(s, zo, g, True)

    def acc_copy(s):
        return remote(acc.at[s], racc.at[k_me], o_ss.at[0, s], o_rs.at[0, k_me],
                      {"ctx_1": lax.div(s, 2), "ctx_2": lax.rem(s, 2)})

    def stat_copy(s):
        return remote(stat.at[s], rstat.at[k_me], o_ss.at[1, s], o_rs.at[1, k_me],
                      {"ctx_1": lax.div(s, 2), "ctx_2": lax.rem(s, 2)})

    @pl.loop(0, 4)
    def _(p):
        @pl.when(p == 1)
        def _():
            k_plus.wait_recv()
            k_on.start()
            v_minus.wait_recv()
            v_on.start()
            v_plus.wait_recv()

        @pl.when(p == 2)
        def _():
            k_minus.wait_recv()

        @pl.when(p == 3)
        def _():
            k_on.wait_recv()
            v_on.wait_recv()

        zo = around(z, jnp.where(p == 1, 3, jnp.where(p == 2, 1, jnp.where(p == 3, 2, 0))))

        @pl.loop(0, 8)
        def _(i):
            s = lax.rem(i + 1 + k_me, 8)
            work(s, zo)

            @pl.when(p == 3)
            def _():
                lane = lax.broadcasted_iota(jnp.int32, (32, 128), 1)
                ms = jnp.full((32, 128), LOW, F32)
                ls = jnp.zeros((32, 128), F32)
                for h in range(16):
                    rows = slice((h % 8) * 32, (h % 8) * 32 + 32)
                    ms = jnp.where(lane == h, m_s[s, h // 8, rows, :], ms)
                    ls = jnp.where(lane == h, l_s[s, h // 8, rows, :], ls)
                stat[s, 0] = ms
                stat[s, 1] = ls

                @pl.when(s != k_me)
                def _():
                    acc_copy(s).start()
                    stat_copy(s).start()

                @pl.when(s == k_me)
                def _():
                    pltpu.make_async_copy(acc.at[s], racc.at[k_me], o_rs.at[0, k_me]).start()
                    pltpu.make_async_copy(stat.at[s], rstat.at[k_me], o_rs.at[1, k_me]).start()

    for i in range(8):
        remote(stat.at[i], rstat.at[i], o_ss.at[1, i], o_rs.at[1, i], at_z(plus)).wait_recv()
        remote(acc.at[i], racc.at[i], o_ss.at[0, i], o_rs.at[0, i], at_z(plus)).wait_recv()

    top = rstat[0, 0]
    for i in range(1, 8):
        top = jnp.maximum(top, rstat[i, 0])
    shares = [jnp.exp2((rstat[i, 0] - top) * EXP2_SCALE) for i in range(8)]
    den = shares[0] * rstat[0, 1]
    for i in range(1, 8):
        den = den + shares[i] * rstat[i, 1]
    for h in range(16):
        rows = slice((h % 8) * 32, (h % 8) * 32 + 32)
        num = shares[0][:, h : h + 1] * racc[0, h // 8, rows, :]
        for i in range(1, 8):
            num = num + shares[i][:, h : h + 1] * racc[i, h // 8, rows, :]
        out_ref[:, h * 128 : (h + 1) * 128] = (num / den[:, h : h + 1]).astype(BF16)

    for i in range(8):
        @pl.when(jnp.logical_not(diagonal & (i == k_me)))
        def _():
            remote(q_hbm, qbuf.at[i], q_ss.at[i], q_rs.at[i], at_z(plus)).wait_send()
        @pl.when(i != k_me)
        def _():
            acc_copy(i).wait_send()
            stat_copy(i).wait_send()
    for c in (k_plus, v_minus, v_plus, k_minus, k_on, v_on):
        c.wait_send()


def attend(q, k, v, loc):
    return pl.pallas_call(
        attend_kernel,
        out_shape=jax.ShapeDtypeStruct((32, 2048), BF16),
        in_specs=[pl.BlockSpec(memory_space=pl.ANY)] * 3 + [pl.BlockSpec(memory_space=pltpu.VMEM)],
        out_specs=pl.BlockSpec(memory_space=pltpu.VMEM),
        scratch_shapes=[
            pltpu.VMEM((8, 32, 2048), BF16),
            pltpu.VMEM((4, 1024, 256), BF16),
            pltpu.VMEM((4, 1024, 256), BF16),
            pltpu.VMEM((8, 2, 256, 1), F32),
            pltpu.VMEM((8, 2, 256, 1), F32),
            pltpu.VMEM((8, 2, 256, 128), F32),
            pltpu.VMEM((8, 2, 32, 128), F32),
            pltpu.VMEM((8, 2, 256, 128), F32),
            pltpu.VMEM((8, 2, 32, 128), F32),
            pltpu.SemaphoreType.DMA((8,)),
            pltpu.SemaphoreType.DMA((8,)),
            pltpu.SemaphoreType.DMA((2,)),
            pltpu.SemaphoreType.DMA((6,)),
            pltpu.SemaphoreType.DMA((6,)),
            pltpu.SemaphoreType.DMA((2, 8)),
            pltpu.SemaphoreType.DMA((2, 8)),
        ],
        compiler_params=pltpu.CompilerParams(
            collective_id=0, has_side_effects=True, vmem_limit_bytes=48 * 1024 * 1024
        ),
        name="attend",
    )(q, k, v, loc)


class Ring:
    def __init__(self, piece, ssem, rsem, base, dev, me):
        self.piece, self.ssem, self.rsem, self.base, self.dev = piece, ssem, rsem, base, dev
        self.plus, self.minus, self.opp = around(me, 1), around(me, 3), around(me, 2)
        self.up = [self.copy(me, h, h, self.plus) for h in range(2)]
        self.down = [self.copy(me, h, 2 + h, self.minus) for h in range(2)]
        self.on_up = self.copy(self.minus, 0, 4, self.plus)
        self.on_down = self.copy(self.plus, 1, 5, self.minus)

    def copy(self, origin, half, n, peer):
        ref = self.piece(origin, half)
        return remote(ref, ref, self.ssem.at[self.base + n], self.rsem.at[self.base + n], self.dev(peer))

    def start(self):
        self.up[0].start()
        self.down[1].start()
        self.up[1].start()
        self.down[0].start()

    def forward(self):
        self.up[0].wait_recv()
        self.on_up.start()
        self.down[1].wait_recv()
        self.on_down.start()

    def near(self):
        self.up[1].wait_recv()
        self.down[0].wait_recv()

    def far(self):
        self.on_up.wait_recv()
        self.on_down.wait_recv()

    def sent(self):
        for c in (*self.up, *self.down, self.on_up, self.on_down):
            c.wait_send()


def run_rings(rings):
    for r in rings:
        r.start()
    for r in rings:
        r.forward()
    for r in rings:
        r.near()
    for r in rings:
        r.far()


class Swap:
    def __init__(self, buf, ssem, rsem, base, dev, me):
        self.copies = [
            remote(buf.at[me], buf.at[me], ssem.at[base + d], rsem.at[base + d], dev(around(me, d)))
            for d in (1, 2, 3)
        ]

    def run(self):
        for c in self.copies:
            c.start()
        for c in self.copies:
            c.wait_recv()

    def sent(self):
        for c in self.copies:
            c.wait_send()


def finish_kernel(
    attn_ref, proj_hbm, skip_ref, gain_ref, lex_hbm, div_ref, tok_ref,
    hidden_ref, logprob_ref,
    rows_all, proj, mixed, from_core, from_y, sq, sq_y, norm, lex, stat, stat_c,
    l_s, s_s, r_s,
):
    z, x, yh = lax.axis_index("ctx_0"), lax.axis_index("ctx_1"), lax.axis_index("ctx_2")
    yl, core = lax.axis_index("head_0"), lax.axis_index("head_1")
    y = 2 * yh + yl
    other = 1 - core

    lex_copy = pltpu.make_async_copy(lex_hbm, lex, l_s.at[0])
    proj_copy = pltpu.make_async_copy(proj_hbm, proj, l_s.at[1])
    proj_copy.start()
    lex_copy.start()

    for d in (1, 2, 3):
        greet(at_z(around(z, d)))
        greet(at_x(around(x, d)))
        greet(at_y(around(y, d)))
    greet(at_core(other))
    pl.semaphore_wait(pltpu.get_barrier_semaphore(), 10)

    pending = []
    count = [0]

    def take(n):
        count[0] += n
        return count[0] - n

    def ring(piece, dev, me):
        r = Ring(piece, s_s, r_s, take(6), dev, me)
        pending.append(r.sent)
        return r

    def single(src, dst, dev):
        n = take(1)
        c = remote(src, dst, s_s.at[n], r_s.at[n], dev)
        pending.append(c.wait_send)
        return c

    def swap(buf, dev, me):
        s = Swap(buf, s_s, r_s, take(4), dev, me)
        pending.append(s.sent)
        s.run()

    rows_all[x, z, yh] = attn_ref[...]
    pair = single(rows_all.at[x, z, yh], rows_all.at[x, z, yh], {"ctx_2": 1 - yh})
    pair.start()
    pair.wait_recv()

    def half_cols(h):
        return pl.ds(h * 1024, 1024)

    lo, hi = pl.ds(0, 16), pl.ds(16, 16)
    run_rings([
        ring(lambda o, h: rows_all.at[x, o, :, lo, half_cols(h)], at_z, z),
        ring(lambda o, h: rows_all.at[o, z, :, hi, half_cols(h)], at_x, x),
    ])
    run_rings([
        ring(lambda o, h: rows_all.at[o, :, :, lo, half_cols(h)], at_x, x),
        ring(lambda o, h: rows_all.at[:, o, :, hi, half_cols(h)], at_z, z),
    ])

    proj_copy.wait()
    w = proj[...]
    for q in range(4):
        a = rows_all[q].reshape(256, 2048)
        mixed[q // 2, q % 2] = jnp.dot(a, w, preferred_element_type=F32)
    c = single(mixed.at[:, other], from_core, at_core(other))
    c.start()
    c.wait_recv()
    mine = mixed.at[:, core]
    for q in range(2):
        from_core[q] = mine[q] + from_core[q]
    c = single(from_core.at[1 - yl], from_y, {"head_0": 1 - yl})
    c.start()
    c.wait_recv()
    hidden = (skip_ref[...].astype(F32) + (from_core[yl] + from_y[...])).astype(BF16)
    hidden_ref[...] = hidden
    wide = hidden.astype(F32)

    part = jnp.sum(jnp.transpose(wide * wide), axis=0, keepdims=True)
    for stage, (dev, me) in enumerate(((at_z, z), (at_x, x))):
        sq[stage, me] = jnp.broadcast_to(part, (8, 256))
        swap(sq.at[stage], dev, me)
        part = sq[stage, 0, 0:1] + sq[stage, 1, 0:1] + sq[stage, 2, 0:1] + sq[stage, 3, 0:1]
    sq_y[yh] = jnp.broadcast_to(part, (8, 256))
    c = single(sq_y.at[yh], sq_y.at[yh], {"ctx_2": 1 - yh})
    c.start()
    c.wait_recv()
    part = sq_y[0, 0:1] + sq_y[1, 0:1]
    factor = jnp.transpose(jnp.broadcast_to(lax.rsqrt(part / D + EPS), (256, 256)))
    norm[z, x, y, core] = (wide * factor * gain_ref[...]).astype(BF16)

    r0, r1, r2 = pl.ds(0, 96), pl.ds(96, 80), pl.ds(176, 80)

    def cols(h):
        return pl.ds(h * 128, 128)

    run_rings([
        ring(lambda o, h: norm.at[o, x, y, core, r0, cols(h)], at_z, z),
        ring(lambda o, h: norm.at[z, o, y, core, r1, cols(h)], at_x, x),
        ring(lambda o, h: norm.at[z, x, o, core, r2, cols(h)], at_y, y),
    ])
    run_rings([
        ring(lambda o, h: norm.at[:, o, y, core, r0, cols(h)], at_x, x),
        ring(lambda o, h: norm.at[z, :, o, core, r1, cols(h)], at_y, y),
        ring(lambda o, h: norm.at[o, x, :, core, r2, cols(h)], at_z, z),
    ])
    last = [
        ring(lambda o, h: norm.at[:, :, o, core, r0, cols(h)], at_y, y),
        ring(lambda o, h: norm.at[o, :, :, core, r1, cols(h)], at_z, z),
        ring(lambda o, h: norm.at[:, o, :, core, r2, cols(h)], at_x, x),
    ]
    parts = [
        lambda o: norm.at[:, :, o, core, r0],
        lambda o: norm.at[o, :, :, core, r1],
        lambda o: norm.at[:, o, :, core, r2],
    ]
    arrivals = []

    def hand_over(ref):
        c = single(ref, ref, at_core(other))
        c.start()
        arrivals.append(c)

    for r in last:
        r.start()
    for f, own in zip(parts, (y, z, x)):
        hand_over(f(own))
    for r in last:
        r.forward()
    for r, f in zip(last, parts):
        r.near()
        hand_over(f(r.plus))
        hand_over(f(r.minus))
    for r, f in zip(last, parts):
        r.far()
        hand_over(f(r.opp))
    for c in arrivals:
        c.wait_recv()
    lex_copy.wait()

    offset = (((z * 4 + x) * 2 + yh) * 4 + yl * 2 + core) * 512
    for group in range(4):
        def add(zz, total):
            a = jnp.concatenate(
                [norm[zz, i // 2, 2 * (i % 2) + group // 2, group % 2] for i in range(8)], axis=1
            )
            first = pl.multiple_of(zz * 2048, 2048)
            return total + jnp.dot(a, lex[pl.ds(first, 2048), :], preferred_element_type=F32)

        rows = slice(group * 256, (group + 1) * 256)
        logits = lax.fori_loop(0, 4, add, jnp.zeros((256, 512), F32)) / div_ref[rows, :]
        ids = lax.broadcasted_iota(jnp.int32, logits.shape, 1) + offset
        picked = jnp.sum(jnp.where(ids == tok_ref[rows, :], logits, 0.0), axis=1, keepdims=True)
        peak = jnp.max(logits, axis=1, keepdims=True)
        total = jnp.sum(jnp.exp(logits - peak), axis=1, keepdims=True)
        lane = lax.broadcasted_iota(jnp.int32, (256, 128), 1)
        both = jnp.where(lane == 0, peak, jnp.where(lane == 1, total, picked))
        stat[0, z, :, rows] = jnp.transpose(both)[0:8, :]

    def joined(tiles):
        peak = tiles[0][0:1]
        for t in tiles[1:]:
            peak = jnp.maximum(peak, t[0:1])
        total = sum(t[1:2] * jnp.exp(t[0:1] - peak) for t in tiles)
        picked = sum(t[2:3] for t in tiles)
        return peak, total, picked

    def spread(values):
        sub = lax.broadcasted_iota(jnp.int32, (8, 1024), 0)
        return jnp.where(sub == 0, values[0], jnp.where(sub == 1, values[1], values[2]))

    values = None
    for stage, (dev, me) in enumerate(((at_z, z), (at_x, x), (at_y, y))):
        if stage:
            stat[stage, me] = spread(values)
        swap(stat.at[stage], dev, me)
        values = joined([stat[stage, i] for i in range(4)])
    stat_c[core] = spread(values)
    c = single(stat_c.at[core], stat_c.at[core], at_core(other))
    c.start()
    c.wait_recv()
    peak, total, picked = joined([stat_c[0], stat_c[1]])
    logprob_ref[...] = picked - peak - jnp.log(total)

    for wait in pending:
        wait()


def finish(attn, proj, skip, gain, lex, div, tok):
    vmem = pl.BlockSpec(memory_space=pltpu.VMEM)
    hbm = pl.BlockSpec(memory_space=pl.ANY)
    return pl.pallas_call(
        finish_kernel,
        out_shape=(
            jax.ShapeDtypeStruct((256, 256), BF16),
            jax.ShapeDtypeStruct((1, 1024), F32),
        ),
        in_specs=[vmem, hbm, vmem, vmem, hbm, vmem, vmem],
        out_specs=(vmem, vmem),
        scratch_shapes=[
            pltpu.VMEM((4, 4, 2, 32, 2048), BF16),
            pltpu.VMEM((2048, 256), BF16),
            pltpu.VMEM((2, 2, 256, 256), F32),
            pltpu.VMEM((2, 256, 256), F32),
            pltpu.VMEM((256, 256), F32),
            pltpu.VMEM((2, 4, 8, 256), F32),
            pltpu.VMEM((2, 8, 256), F32),
            pltpu.VMEM((4, 4, 4, 2, 256, 256), BF16),
            pltpu.VMEM((8192, 512), BF16),
            pltpu.VMEM((3, 4, 8, 1024), F32),
            pltpu.VMEM((2, 8, 1024), F32),
            pltpu.SemaphoreType.DMA((2,)),
            pltpu.SemaphoreType.DMA((128,)),
            pltpu.SemaphoreType.DMA((128,)),
        ],
        compiler_params=pltpu.CompilerParams(
            collective_id=1, has_side_effects=True, vmem_limit_bytes=56 * 1024 * 1024
        ),
        name="finish",
    )(attn, proj, skip, gain, lex, div, tok)


def shards(q, k, v, loc, proj, skip, gain, lex, div, tok):
    attn = attend(q, k, v, loc.reshape(1024, 1))
    hidden, logprob = finish(
        attn, proj, skip, gain.reshape(1, 256), lex, div.reshape(1024, 1), tok.reshape(1024, 1)
    )
    return hidden, logprob.reshape(1024)


def solution(mesh):
    torus = Mesh(mesh.devices.reshape(4, 4, 2, 2, 2), CTX_HEAD)
    placed = (
        P(CTX, HEAD),
        P(CTX, HEAD),
        P(CTX, HEAD),
        P(),
        P(HEAD, CTX),
        P(HEAD, CTX),
        P(CTX),
        P(None, CTX_HEAD),
        P(),
        P(),
    )
    return jax.shard_map(
        shards, mesh=torus, in_specs=placed, out_specs=(P(HEAD, CTX), P()), check_vma=False
    )
```

```python
import jax
import jax.numpy as jnp
from jax import lax
from jax.experimental import pallas as pl
from jax.experimental.pallas import tpu as pltpu
from jax.sharding import Mesh
from jax.sharding import PartitionSpec as P

D = 8192
EPS = 1e-05
LOW = -1e30
LOG2E = 1.4426950408889634
EXP2_SCALE = 128 ** (-0.5) * LOG2E
CTX = ("ctx_0", "ctx_1", "ctx_2")
HEAD = ("head_0", "head_1")
CTX_HEAD = CTX + HEAD
F32 = jnp.float32
BF16 = jnp.bfloat16
MESH = pl.DeviceIdType.MESH


def at_z(p):
    return {"ctx_0": p}


def at_x(p):
    return {"ctx_1": p}


def at_y(p):
    return {"ctx_2": lax.div(p, 2), "head_0": lax.rem(p, 2)}


def at_core(p):
    return {"head_1": p}


def around(p, d):
    return lax.rem(p + d, 4)


def remote(src, dst, ssem, rsem, dev):
    return pltpu.make_async_remote_copy(
        src_ref=src, dst_ref=dst, send_sem=ssem, recv_sem=rsem, device_id=dev, device_id_type=MESH
    )


def greet(dev):
    pl.semaphore_signal(pltpu.get_barrier_semaphore(), inc=1, device_id=dev, device_id_type=MESH)


class Ring:
    def __init__(self, piece, ssem, rsem, base, dev, me):
        self.piece, self.ssem, self.rsem, self.base, self.dev = piece, ssem, rsem, base, dev
        self.plus, self.minus, self.opp = around(me, 1), around(me, 3), around(me, 2)
        self.up = [self.copy(me, h, h, self.plus) for h in range(2)]
        self.down = [self.copy(me, h, 2 + h, self.minus) for h in range(2)]
        self.on_up = self.copy(self.minus, 0, 4, self.plus)
        self.on_down = self.copy(self.plus, 1, 5, self.minus)

    def copy(self, origin, half, n, peer):
        ref = self.piece(origin, half)
        return remote(ref, ref, self.ssem.at[self.base + n], self.rsem.at[self.base + n], self.dev(peer))

    def start(self):
        self.up[0].start()
        self.down[1].start()
        self.up[1].start()
        self.down[0].start()

    def forward(self):
        self.up[0].wait_recv()
        self.on_up.start()
        self.down[1].wait_recv()
        self.on_down.start()

    def near(self):
        self.up[1].wait_recv()
        self.down[0].wait_recv()

    def far(self):
        self.on_up.wait_recv()
        self.on_down.wait_recv()

    def sent(self):
        for c in (*self.up, *self.down, self.on_up, self.on_down):
            c.wait_send()


def run_rings(rings):
    for r in rings:
        r.start()
    for r in rings:
        r.forward()
    for r in rings:
        r.near()
    for r in rings:
        r.far()


class Swap:
    def __init__(self, buf, ssem, rsem, base, dev, me):
        self.copies = [
            remote(buf.at[me], buf.at[me], ssem.at[base + d], rsem.at[base + d], dev(around(me, d)))
            for d in (1, 2, 3)
        ]

    def run(self):
        for c in self.copies:
            c.start()
        for c in self.copies:
            c.wait_recv()

    def sent(self):
        for c in self.copies:
            c.wait_send()


def column(row):
    return jnp.transpose(jnp.broadcast_to(row, (128, row.shape[1])))[:, 0:1]


def kernel(
    q_hbm, k_hbm, v_hbm, loc_ref, proj_hbm, skip_ref, gain_ref, lex_hbm, div_ref, tok_ref,
    hidden_ref, logprob_ref,
    qbuf, kbuf, vbuf, loc_col, m_s, l_s, acc, part_stat, racc, rstat,
    rows_all, proj, mixed, from_core, from_y, sq, sq_y, norm, lex, stat, stat_c,
    l_sem, s_s, r_s,
):
    z, x, yh = lax.axis_index("ctx_0"), lax.axis_index("ctx_1"), lax.axis_index("ctx_2")
    yl, core = lax.axis_index("head_0"), lax.axis_index("head_1")
    y = 2 * yh + yl
    other, mate = 1 - core, 1 - yh
    diagonal = x == z

    proj_copy = pltpu.make_async_copy(proj_hbm, proj, l_sem.at[0])
    lex_copy = pltpu.make_async_copy(lex_hbm, lex, l_sem.at[1])

    def head_cols(ref, g):
        return ref.at[:, pl.ds(pl.multiple_of(g * 128, 128), 128)]

    own_k = pltpu.make_async_copy(head_cols(k_hbm, yh), kbuf.at[z, yh], l_sem.at[2])
    own_v = pltpu.make_async_copy(head_cols(v_hbm, yh), vbuf.at[z, yh], l_sem.at[3])
    own_k.start()
    own_v.start()

    for d in (1, 2, 3):
        greet(at_z(around(z, d)))
        greet(at_x(around(x, d)))
        greet(at_y(around(y, d)))
    greet(at_core(other))
    for i in range(2):
        @pl.when(jnp.logical_not(diagonal & (i == yh)))
        def _():
            greet({"ctx_0": x, "ctx_1": z, "ctx_2": i})
    pl.semaphore_wait(pltpu.get_barrier_semaphore(), 10 + jnp.where(diagonal, 1, 2))

    pending = []
    count = [0]

    def take(n):
        count[0] += n
        return count[0] - n

    def ring(piece, dev, me):
        r = Ring(piece, s_s, r_s, take(6), dev, me)
        pending.append(r.sent)
        return r

    def single(src, dst, dev):
        n = take(1)
        c = remote(src, dst, s_s.at[n], r_s.at[n], dev)
        pending.append(c.wait_send)
        return c

    def swap(buf, dev, me):
        s = Swap(buf, s_s, r_s, take(4), dev, me)
        pending.append(s.sent)
        s.run()

    q_at = take(2)

    def q_copies(i):
        src = q_hbm.at[:, i * 1024 : (i + 1) * 1024]
        dst = qbuf.at[z, pl.ds(pl.multiple_of(yh * 32, 32), 32)]
        return src, dst

    def q_send(i):
        peer = {"ctx_0": x, "ctx_1": z, "ctx_2": i}
        return remote(*q_copies(i), s_s.at[q_at + i], r_s.at[q_at + yh], peer)

    for i in range(2):
        to_self = diagonal & (i == yh)
        @pl.when(jnp.logical_not(to_self))
        def _():
            q_send(i).start()
        @pl.when(to_self)
        def _():
            pltpu.make_async_copy(*q_copies(i), r_s.at[q_at + yh]).start()

    k_swap = single(head_cols(k_hbm, mate), kbuf.at[z, yh], {"ctx_2": mate})
    v_swap = single(head_cols(v_hbm, mate), vbuf.at[z, yh], {"ctx_2": mate})
    k_swap.start()
    v_swap.start()

    def kv_ring(yo):
        return ring(lambda o, h: (vbuf if h else kbuf).at[o, yo], at_z, z)

    own_ring, mate_ring = kv_ring(yh), kv_ring(mate)
    own_k.wait()
    own_v.wait()
    own_ring.start()

    m_s[...] = jnp.full(m_s.shape, LOW, F32)
    l_s[...] = jnp.zeros(l_s.shape, F32)
    acc[...] = jnp.zeros(acc.shape, F32)
    for i in range(8):
        cols = slice(i * 128, (i + 1) * 128)
        loc_col[cols, :] = jnp.transpose(jnp.broadcast_to(loc_ref[:, cols], (128, 128)))

    for i in range(2):
        dst = qbuf.at[x, i * 32 : (i + 1) * 32]
        remote(dst, dst, s_s.at[q_at], r_s.at[q_at + i], at_x(around(x, 1))).wait_recv()
    q_ring = ring(lambda o, h: qbuf.at[o, :, h * 512 : (h + 1) * 512], at_x, x)
    q_ring.start()
    k_swap.wait_recv()
    v_swap.wait_recv()
    mate_ring.start()
    q_ring.forward()
    proj_copy.start()
    q_ring.near()
    q_ring.far()

    def tile(s, c, zo, yo, masked):
        q = jnp.concatenate(
            [qbuf[s, c * 32 : (c + 1) * 32, j * 128 : (j + 1) * 128] for j in range(8)], axis=0
        )
        raw = lax.dot_general(
            q, kbuf[zo, yo], (((1,), (1,)), ((), ())), preferred_element_type=F32
        )
        if masked:
            base = 8 * zo + 2 * x + yo
            first = pl.multiple_of(base * 32, 32)
            loc = loc_col[pl.ds(first, 32), 0:1] - base * 1024
            loc = jnp.concatenate([loc] * 8, axis=0)
            pos = lax.broadcasted_iota(jnp.int32, raw.shape, 1)
            raw = jnp.where(pos <= loc, raw, LOW)
        top = jnp.max(raw, axis=1, keepdims=True)
        w = jnp.exp2((raw - top) * EXP2_SCALE)
        total = jnp.sum(w, axis=1, keepdims=True)
        part = jnp.dot(w.astype(BF16), vbuf[zo, yo], preferred_element_type=F32)
        m_old = m_s[s, c]
        m_new = jnp.maximum(m_old, top)
        a = jnp.exp2((m_old - m_new) * EXP2_SCALE)
        b = jnp.exp2((top - m_new) * EXP2_SCALE)
        m_s[s, c] = m_new
        l_s[s, c] = l_s[s, c] * a + total * b
        acc[s, c] = acc[s, c] * a + part * b

    def work(s, zo, yo):
        chunk = 8 * s + 2 * z
        block = 8 * zo + 2 * x + yo

        @pl.when(chunk > block)
        def _():
            tile(s, 0, zo, yo, False)
            tile(s, 1, zo, yo, False)

        @pl.when(chunk == block)
        def _():
            tile(s, 0, zo, yo, True)
            tile(s, 1, zo, yo, False)

        @pl.when(chunk + 1 == block)
        def _():
            tile(s, 1, zo, yo, True)

    part_at = take(8)

    def acc_copy(s):
        return remote(acc.at[s], racc.at[x], s_s.at[part_at + s], r_s.at[part_at + x], at_x(s))

    def stat_copy(s):
        return remote(part_stat.at[s], rstat.at[x], s_s.at[part_at + 4 + s],
                      r_s.at[part_at + 4 + x], at_x(s))

    @pl.loop(0, 8)
    def _(p):
        @pl.when(p == 2)
        def _():
            own_ring.forward()
            own_ring.up[1].wait_recv()

        @pl.when(p == 3)
        def _():
            own_ring.down[0].wait_recv()

        @pl.when(p == 4)
        def _():
            mate_ring.forward()
            mate_ring.up[1].wait_recv()

        @pl.when(p == 5)
        def _():
            mate_ring.down[0].wait_recv()

        @pl.when(p == 6)
        def _():
            own_ring.far()

        @pl.when(p == 7)
        def _():
            mate_ring.far()

        step = jnp.where(p < 2, 0, jnp.where(p >= 6, 2, jnp.where(lax.rem(p, 2) == 0, 3, 1)))
        is_own = (p == 0) | (p == 2) | (p == 3) | (p == 6)
        zo = around(z, step)
        yo = jnp.where(is_own, yh, mate)

        @pl.loop(0, 4)
        def _(i):
            s = around(x, jnp.where(i == 0, 2, jnp.where(i == 1, 1, jnp.where(i == 2, 3, 0))))
            work(s, zo, yo)

            @pl.when(p == 7)
            def _():
                lane = lax.broadcasted_iota(jnp.int32, (32, 128), 1)
                for c in range(2):
                    t = jnp.zeros((32, 128), F32)
                    for j in range(8):
                        rows = slice(j * 32, (j + 1) * 32)
                        t = jnp.where(lane == j, m_s[s, c, rows, :], t)
                        t = jnp.where(lane == 8 + j, l_s[s, c, rows, :], t)
                    part_stat[s, c] = t

                @pl.when(s != x)
                def _():
                    acc_copy(s).start()
                    stat_copy(s).start()

                @pl.when(s == x)
                def _():
                    pltpu.make_async_copy(acc.at[s], racc.at[x], r_s.at[part_at + x]).start()
                    pltpu.make_async_copy(part_stat.at[s], rstat.at[x], r_s.at[part_at + 4 + x]).start()

    lex_copy.start()
    for i in range(4):
        remote(part_stat.at[i], rstat.at[i], s_s.at[part_at + 4 + i], r_s.at[part_at + 4 + i],
               at_x(around(x, 1))).wait_recv()
        remote(acc.at[i], racc.at[i], s_s.at[part_at + i], r_s.at[part_at + i],
               at_x(around(x, 1))).wait_recv()

    for c in range(2):
        tops = [rstat[i, c] for i in range(4)]
        sums = [pltpu.roll(t, 120, 1) for t in tops]
        top = jnp.maximum(jnp.maximum(tops[0], tops[1]), jnp.maximum(tops[2], tops[3]))
        shares = [jnp.exp2((t - top) * EXP2_SCALE) for t in tops]
        den = sum(a * b for a, b in zip(shares, sums))
        joined_rows = []
        for j in range(8):
            rows = slice(j * 32, (j + 1) * 32)
            num = sum(shares[i][:, j : j + 1] * racc[i, c, rows, :] for i in range(4))
            joined_rows.append((num / den[:, j : j + 1]).astype(BF16))
        rows_all[x, z, c * 32 : (c + 1) * 32, pl.ds(pl.multiple_of(yh * 1024, 1024), 1024)] = (
            jnp.concatenate(joined_rows, axis=1)
        )
    for i in range(4):
        @pl.when(i != x)
        def _():
            acc_copy(i).wait_send()
            stat_copy(i).wait_send()
    for i in range(2):
        @pl.when(jnp.logical_not(diagonal & (i == yh)))
        def _():
            q_send(i).wait_send()

    own_cols = pl.ds(pl.multiple_of(yh * 1024, 1024), 1024)
    pair = single(rows_all.at[x, z, :, own_cols], rows_all.at[x, z, :, own_cols], {"ctx_2": mate})
    pair.start()
    pair.wait_recv()

    def half_cols(h):
        return pl.ds(h * 1024, 1024)

    lo, hi = pl.ds(0, 32), pl.ds(32, 32)
    run_rings([
        ring(lambda o, h: rows_all.at[x, o, lo, half_cols(h)], at_z, z),
        ring(lambda o, h: rows_all.at[o, z, hi, half_cols(h)], at_x, x),
    ])
    run_rings([
        ring(lambda o, h: rows_all.at[o, :, lo, half_cols(h)], at_x, x),
        ring(lambda o, h: rows_all.at[:, o, hi, half_cols(h)], at_z, z),
    ])

    proj_copy.wait()
    w = proj[...]
    for q in range(4):
        a = rows_all[q].reshape(256, 2048)
        mixed[q // 2, q % 2] = jnp.dot(a, w, preferred_element_type=F32)
    c = single(mixed.at[:, other], from_core, at_core(other))
    c.start()
    c.wait_recv()
    mine = mixed.at[:, core]
    for q in range(2):
        from_core[q] = mine[q] + from_core[q]
    c = single(from_core.at[1 - yl], from_y, {"head_0": 1 - yl})
    c.start()
    c.wait_recv()
    hidden = (skip_ref[...].astype(F32) + (from_core[yl] + from_y[...])).astype(BF16)
    hidden_ref[...] = hidden
    wide = hidden.astype(F32)

    part = jnp.sum(jnp.transpose(wide * wide), axis=0, keepdims=True)
    for stage, (dev, me) in enumerate(((at_z, z), (at_x, x))):
        sq[stage, me] = jnp.broadcast_to(part, (8, 256))
        swap(sq.at[stage], dev, me)
        part = sq[stage, 0, 0:1] + sq[stage, 1, 0:1] + sq[stage, 2, 0:1] + sq[stage, 3, 0:1]
    sq_y[yh] = jnp.broadcast_to(part, (8, 256))
    c = single(sq_y.at[yh], sq_y.at[yh], {"ctx_2": 1 - yh})
    c.start()
    c.wait_recv()
    part = sq_y[0, 0:1] + sq_y[1, 0:1]
    factor = jnp.transpose(jnp.broadcast_to(lax.rsqrt(part / D + EPS), (256, 256)))
    norm[z, x, y, core] = (wide * factor * gain_ref[...]).astype(BF16)

    r0, r1, r2 = pl.ds(0, 96), pl.ds(96, 80), pl.ds(176, 80)

    def cols(h):
        return pl.ds(h * 128, 128)

    run_rings([
        ring(lambda o, h: norm.at[o, x, y, core, r0, cols(h)], at_z, z),
        ring(lambda o, h: norm.at[z, o, y, core, r1, cols(h)], at_x, x),
        ring(lambda o, h: norm.at[z, x, o, core, r2, cols(h)], at_y, y),
    ])
    run_rings([
        ring(lambda o, h: norm.at[:, o, y, core, r0, cols(h)], at_x, x),
        ring(lambda o, h: norm.at[z, :, o, core, r1, cols(h)], at_y, y),
        ring(lambda o, h: norm.at[o, x, :, core, r2, cols(h)], at_z, z),
    ])
    last = [
        ring(lambda o, h: norm.at[:, :, o, core, r0, cols(h)], at_y, y),
        ring(lambda o, h: norm.at[o, :, :, core, r1, cols(h)], at_z, z),
        ring(lambda o, h: norm.at[:, o, :, core, r2, cols(h)], at_x, x),
    ]
    parts = [
        lambda o: norm.at[:, :, o, core, r0],
        lambda o: norm.at[o, :, :, core, r1],
        lambda o: norm.at[:, o, :, core, r2],
    ]
    arrivals = []

    def hand_over(ref):
        c = single(ref, ref, at_core(other))
        c.start()
        arrivals.append(c)

    for r in last:
        r.start()
    for f, own in zip(parts, (y, z, x)):
        hand_over(f(own))
    for r in last:
        r.forward()
    for r, f in zip(last, parts):
        r.near()
        hand_over(f(r.plus))
        hand_over(f(r.minus))
    for r, f in zip(last, parts):
        r.far()
        hand_over(f(r.opp))
    for c in arrivals:
        c.wait_recv()
    lex_copy.wait()

    offset = (((z * 4 + x) * 2 + yh) * 4 + yl * 2 + core) * 512
    for group in range(4):
        def add(zz, total):
            a = jnp.concatenate(
                [norm[zz, i // 2, 2 * (i % 2) + group // 2, group % 2] for i in range(8)], axis=1
            )
            first = pl.multiple_of(zz * 2048, 2048)
            return total + jnp.dot(a, lex[pl.ds(first, 2048), :], preferred_element_type=F32)

        rows = slice(group * 256, (group + 1) * 256)
        logits = lax.fori_loop(0, 4, add, jnp.zeros((256, 512), F32)) / column(div_ref[:, rows])
        ids = lax.broadcasted_iota(jnp.int32, logits.shape, 1) + offset
        picked = jnp.sum(jnp.where(ids == column(tok_ref[:, rows]), logits, 0.0), axis=1, keepdims=True)
        peak = jnp.max(logits, axis=1, keepdims=True)
        total = jnp.sum(jnp.exp(logits - peak), axis=1, keepdims=True)
        lane = lax.broadcasted_iota(jnp.int32, (256, 128), 1)
        both = jnp.where(lane == 0, peak, jnp.where(lane == 1, total, picked))
        stat[0, z, :, rows] = jnp.transpose(both)[0:8, :]

    def joined(tiles):
        peak = tiles[0][0:1]
        for t in tiles[1:]:
            peak = jnp.maximum(peak, t[0:1])
        total = sum(t[1:2] * jnp.exp(t[0:1] - peak) for t in tiles)
        picked = sum(t[2:3] for t in tiles)
        return peak, total, picked

    def spread(values):
        sub = lax.broadcasted_iota(jnp.int32, (8, 1024), 0)
        return jnp.where(sub == 0, values[0], jnp.where(sub == 1, values[1], values[2]))

    values = None
    for stage, (dev, me) in enumerate(((at_z, z), (at_x, x), (at_y, y))):
        if stage:
            stat[stage, me] = spread(values)
        swap(stat.at[stage], dev, me)
        values = joined([stat[stage, i] for i in range(4)])
    stat_c[core] = spread(values)
    c = single(stat_c.at[core], stat_c.at[core], at_core(other))
    c.start()
    c.wait_recv()
    peak, total, picked = joined([stat_c[0], stat_c[1]])
    logprob_ref[...] = picked - peak - jnp.log(total)

    for wait in pending:
        wait()


def whole(q, k, v, loc, proj, skip, gain, lex, div, tok):
    vmem = pl.BlockSpec(memory_space=pltpu.VMEM)
    hbm = pl.BlockSpec(memory_space=pl.ANY)
    return pl.pallas_call(
        kernel,
        out_shape=(
            jax.ShapeDtypeStruct((256, 256), BF16),
            jax.ShapeDtypeStruct((1, 1024), F32),
        ),
        in_specs=[hbm, hbm, hbm, vmem, hbm, vmem, vmem, hbm, vmem, vmem],
        out_specs=(vmem, vmem),
        scratch_shapes=[
            pltpu.VMEM((4, 64, 1024), BF16),
            pltpu.VMEM((4, 2, 1024, 128), BF16),
            pltpu.VMEM((4, 2, 1024, 128), BF16),
            pltpu.VMEM((1024, 128), jnp.int32),
            pltpu.VMEM((4, 2, 256, 1), F32),
            pltpu.VMEM((4, 2, 256, 1), F32),
            pltpu.VMEM((4, 2, 256, 128), F32),
            pltpu.VMEM((4, 2, 32, 128), F32),
            pltpu.VMEM((4, 2, 256, 128), F32),
            pltpu.VMEM((4, 2, 32, 128), F32),
            pltpu.VMEM((4, 4, 64, 2048), BF16),
            pltpu.VMEM((2048, 256), BF16),
            pltpu.VMEM((2, 2, 256, 256), F32),
            pltpu.VMEM((2, 256, 256), F32),
            pltpu.VMEM((256, 256), F32),
            pltpu.VMEM((2, 4, 8, 256), F32),
            pltpu.VMEM((2, 8, 256), F32),
            pltpu.VMEM((4, 4, 4, 2, 256, 256), BF16),
            pltpu.VMEM((8192, 512), BF16),
            pltpu.VMEM((3, 4, 8, 1024), F32),
            pltpu.VMEM((2, 8, 1024), F32),
            pltpu.SemaphoreType.DMA((4,)),
            pltpu.SemaphoreType.DMA((160,)),
            pltpu.SemaphoreType.DMA((160,)),
        ],
        compiler_params=pltpu.CompilerParams(
            collective_id=0, has_side_effects=True, vmem_limit_bytes=58 * 1024 * 1024
        ),
        name="whole",
    )(q, k, v, loc, proj, skip, gain, lex, div, tok)


def shards(q, k, v, loc, proj, skip, gain, lex, div, tok):
    hidden, logprob = whole(
        q, k, v, loc.reshape(1, 1024), proj, skip, gain.reshape(1, 256), lex,
        div.reshape(1, 1024), tok.reshape(1, 1024)
    )
    return hidden, logprob.reshape(1024)


def solution(mesh):
    torus = Mesh(mesh.devices.reshape(4, 4, 2, 2, 2), CTX_HEAD)
    placed = (
        P(CTX, HEAD),
        P(CTX, HEAD),
        P(CTX, HEAD),
        P(),
        P(HEAD, CTX),
        P(HEAD, CTX),
        P(CTX),
        P(None, CTX_HEAD),
        P(),
        P(),
    )
    return jax.shard_map(
        shards, mesh=torus, in_specs=placed, out_specs=(P(HEAD, CTX), P()), check_vma=False
    )
```

```python
import jax
import jax.numpy as jnp
from jax import lax
from jax.experimental import pallas as pl
from jax.experimental.pallas import tpu as pltpu
from jax.sharding import Mesh
from jax.sharding import PartitionSpec as P

D = 8192
EPS = 1e-05
LOW = -1e30
GROUPS = 2
LOG2E = 1.4426950408889634
EXP2_SCALE = 128 ** (-0.5) * LOG2E
CTX = ("ctx_0", "ctx_1", "ctx_2")
HEAD = ("head_0", "head_1")
CTX_HEAD = CTX + HEAD
F32 = jnp.float32
BF16 = jnp.bfloat16
MESH = pl.DeviceIdType.MESH


def at_z(p):
    return {"ctx_0": p}


def at_x(p):
    return {"ctx_1": p}


def at_y(p):
    return {"ctx_2": lax.div(p, 2), "head_0": lax.rem(p, 2)}


def at_core(p):
    return {"head_1": p}


def around(p, d):
    return lax.rem(p + d, 4)


def remote(src, dst, ssem, rsem, dev):
    return pltpu.make_async_remote_copy(
        src_ref=src, dst_ref=dst, send_sem=ssem, recv_sem=rsem, device_id=dev, device_id_type=MESH
    )


def greet(dev):
    pl.semaphore_signal(pltpu.get_barrier_semaphore(), inc=1, device_id=dev, device_id_type=MESH)


class Ring:
    def __init__(self, piece, ssem, rsem, base, dev, me):
        self.piece, self.ssem, self.rsem, self.base, self.dev = piece, ssem, rsem, base, dev
        self.plus, self.minus, self.opp = around(me, 1), around(me, 3), around(me, 2)
        self.up = [self.copy(me, h, h, self.plus) for h in range(2)]
        self.down = [self.copy(me, h, 2 + h, self.minus) for h in range(2)]
        self.on_up = self.copy(self.minus, 0, 4, self.plus)
        self.on_down = self.copy(self.plus, 1, 5, self.minus)

    def copy(self, origin, half, n, peer):
        ref = self.piece(origin, half)
        return remote(ref, ref, self.ssem.at[self.base + n], self.rsem.at[self.base + n], self.dev(peer))

    def start(self):
        self.up[0].start()
        self.down[1].start()
        self.up[1].start()
        self.down[0].start()

    def forward(self):
        self.up[0].wait_recv()
        self.on_up.start()
        self.down[1].wait_recv()
        self.on_down.start()

    def near(self):
        self.up[1].wait_recv()
        self.down[0].wait_recv()

    def far(self):
        self.on_up.wait_recv()
        self.on_down.wait_recv()

    def sent(self):
        for c in (*self.up, *self.down, self.on_up, self.on_down):
            c.wait_send()


def run_rings(rings):
    for r in rings:
        r.start()
    for r in rings:
        r.forward()
    for r in rings:
        r.near()
    for r in rings:
        r.far()


class Swap:
    def __init__(self, buf, ssem, rsem, base, dev, me):
        self.copies = [
            remote(buf.at[me], buf.at[me], ssem.at[base + d], rsem.at[base + d], dev(around(me, d)))
            for d in (1, 2, 3)
        ]

    def run(self):
        for c in self.copies:
            c.start()
        for c in self.copies:
            c.wait_recv()

    def sent(self):
        for c in self.copies:
            c.wait_send()


def column(row):
    return jnp.transpose(jnp.broadcast_to(row, (128, row.shape[1])))[:, 0:1]


def kernel(
    q_hbm, k_hbm, v_hbm, loc_ref, proj_hbm, skip_ref, gain_ref, lex_hbm, div_ref, tok_ref,
    hidden_ref, logprob_ref,
    qbuf, kbuf, vbuf, loc_col, m_s, l_s, acc, part_stat, racc, rstat,
    rows_all, proj, mixed, from_core, from_y, skip, gain, back, sq_c, sq, norm, lex, logit, stat, stat_c,
    l_sem, s_s, r_s,
):
    z, x, yh = lax.axis_index("ctx_0"), lax.axis_index("ctx_1"), lax.axis_index("ctx_2")
    yl, core = lax.axis_index("head_0"), lax.axis_index("head_1")
    y = 2 * yh + yl
    other, mate = 1 - core, 1 - yh
    diagonal = x == z
    head = 2 * yl + core
    twin = {"ctx_1": head, "head_0": lax.div(x, 2), "head_1": lax.rem(x, 2)}
    is_twin = x == head

    proj_copy = pltpu.make_async_copy(proj_hbm, proj.at[x], l_sem.at[0])
    lex_copy = pltpu.make_async_copy(lex_hbm, lex, l_sem.at[1])

    def head_cols(ref, g):
        return ref.at[:, pl.ds(pl.multiple_of(g * 128, 128), 128)]

    own_k = pltpu.make_async_copy(head_cols(k_hbm, yh), kbuf.at[z, yh], l_sem.at[2])
    own_v = pltpu.make_async_copy(head_cols(v_hbm, yh), vbuf.at[z, yh], l_sem.at[3])
    own_k.start()
    own_v.start()
    proj_copy.start()

    for d in (1, 2, 3):
        greet(at_z(around(z, d)))
        greet(at_x(around(x, d)))
        greet(at_y(around(y, d)))
        for e in (1, 2, 3):
            greet({**at_z(around(z, d)), **at_y(around(y, e))})
    greet(at_core(other))
    for i in range(2):
        @pl.when(jnp.logical_not(diagonal & (i == yh)))
        def _():
            greet({"ctx_0": x, "ctx_1": z, "ctx_2": i})
    @pl.when(jnp.logical_not(is_twin))
    def _():
        greet(twin)
    pl.semaphore_wait(
        pltpu.get_barrier_semaphore(), 19 + jnp.where(diagonal, 1, 2) + jnp.where(is_twin, 0, 1)
    )

    pending = []
    count = [0]

    def take(n):
        count[0] += n
        return count[0] - n

    def ring(piece, dev, me):
        r = Ring(piece, s_s, r_s, take(6), dev, me)
        pending.append(r.sent)
        return r

    def single(src, dst, dev):
        n = take(1)
        c = remote(src, dst, s_s.at[n], r_s.at[n], dev)
        pending.append(c.wait_send)
        return c

    def swap(buf, dev, me):
        s = Swap(buf, s_s, r_s, take(4), dev, me)
        pending.append(s.sent)
        s.run()

    def to_twin(src, dst, n):
        @pl.when(is_twin)
        def _():
            pltpu.make_async_copy(src, dst, r_s.at[n]).start()
        @pl.when(jnp.logical_not(is_twin))
        def _():
            remote(src, dst, s_s.at[n], r_s.at[n], twin).start()

    def from_twin(src, dst, n):
        remote(src, dst, s_s.at[n], r_s.at[n], twin).wait_recv()

    def twin_sent(src, dst, n):
        @pl.when(jnp.logical_not(is_twin))
        def _():
            remote(src, dst, s_s.at[n], r_s.at[n], twin).wait_send()

    q_at = take(2)

    def q_copies(i):
        src = q_hbm.at[:, i * 1024 : (i + 1) * 1024]
        dst = qbuf.at[z, pl.ds(pl.multiple_of(yh * 32, 32), 32)]
        return src, dst

    def q_send(i):
        peer = {"ctx_0": x, "ctx_1": z, "ctx_2": i}
        return remote(*q_copies(i), s_s.at[q_at + i], r_s.at[q_at + yh], peer)

    for i in range(2):
        to_self = diagonal & (i == yh)
        @pl.when(jnp.logical_not(to_self))
        def _():
            q_send(i).start()
        @pl.when(to_self)
        def _():
            pltpu.make_async_copy(*q_copies(i), r_s.at[q_at + yh]).start()

    k_swap = single(head_cols(k_hbm, mate), kbuf.at[z, yh], {"ctx_2": mate})
    v_swap = single(head_cols(v_hbm, mate), vbuf.at[z, yh], {"ctx_2": mate})
    k_swap.start()
    v_swap.start()

    def kv_ring(yo):
        return ring(lambda o, h: (vbuf if h else kbuf).at[o, yo], at_z, z)

    own_ring, mate_ring = kv_ring(yh), kv_ring(mate)
    own_k.wait()
    own_v.wait()
    own_ring.start()

    m_s[...] = jnp.full(m_s.shape, LOW, F32)
    l_s[...] = jnp.zeros(l_s.shape, F32)
    acc[...] = jnp.zeros(acc.shape, F32)
    for i in range(8):
        cols = slice(i * 128, (i + 1) * 128)
        loc_col[cols, :] = jnp.transpose(jnp.broadcast_to(loc_ref[:, cols], (128, 128)))

    for i in range(2):
        dst = qbuf.at[x, i * 32 : (i + 1) * 32]
        remote(dst, dst, s_s.at[q_at], r_s.at[q_at + i], at_x(around(x, 1))).wait_recv()
    q_ring = ring(lambda o, h: qbuf.at[o, :, h * 512 : (h + 1) * 512], at_x, x)
    q_ring.start()
    own_ring.forward()
    q_ring.forward()

    proj_copy.wait()
    proj_ring = ring(lambda o, h: proj.at[o, h * 1024 : (h + 1) * 1024], at_x, x)
    proj_ring.start()
    k_swap.wait_recv()
    v_swap.wait_recv()
    mate_ring.start()
    q_ring.near()
    q_ring.far()
    skip_at = take(2)
    to_twin(skip_ref, skip, skip_at)
    to_twin(gain_ref, gain, skip_at + 1)

    def tile(s, c, zo, yo, masked):
        q = jnp.concatenate(
            [qbuf[s, c * 32 : (c + 1) * 32, j * 128 : (j + 1) * 128] for j in range(8)], axis=0
        )
        raw = lax.dot_general(
            q, kbuf[zo, yo], (((1,), (1,)), ((), ())), preferred_element_type=F32
        )
        if masked:
            base = 8 * zo + 2 * x + yo
            first = pl.multiple_of(base * 32, 32)
            loc = loc_col[pl.ds(first, 32), 0:1] - base * 1024
            loc = jnp.concatenate([loc] * 8, axis=0)
            pos = lax.broadcasted_iota(jnp.int32, raw.shape, 1)
            raw = jnp.where(pos <= loc, raw, LOW)
        top = jnp.max(raw, axis=1, keepdims=True)
        w = jnp.exp2((raw - top) * EXP2_SCALE)
        total = jnp.sum(w, axis=1, keepdims=True)
        part = jnp.dot(w.astype(BF16), vbuf[zo, yo], preferred_element_type=F32)
        m_old = m_s[s, c]
        m_new = jnp.maximum(m_old, top)
        a = jnp.exp2((m_old - m_new) * EXP2_SCALE)
        b = jnp.exp2((top - m_new) * EXP2_SCALE)
        m_s[s, c] = m_new
        l_s[s, c] = l_s[s, c] * a + total * b
        acc[s, c] = acc[s, c] * a + part * b

    def work(s, zo, yo):
        chunk = 8 * s + 2 * z
        block = 8 * zo + 2 * x + yo

        @pl.when(chunk > block)
        def _():
            tile(s, 0, zo, yo, False)
            tile(s, 1, zo, yo, False)

        @pl.when(chunk == block)
        def _():
            tile(s, 0, zo, yo, True)
            tile(s, 1, zo, yo, False)

        @pl.when(chunk + 1 == block)
        def _():
            tile(s, 1, zo, yo, True)

    part_at = take(8)

    def acc_copy(s):
        return remote(acc.at[s], racc.at[x], s_s.at[part_at + s], r_s.at[part_at + x], at_x(s))

    def stat_copy(s):
        return remote(part_stat.at[s], rstat.at[x], s_s.at[part_at + 4 + s],
                      r_s.at[part_at + 4 + x], at_x(s))

    @pl.loop(0, 8)
    def _(p):
        @pl.when(p == 2)
        def _():
            own_ring.up[1].wait_recv()

        @pl.when(p == 3)
        def _():
            own_ring.down[0].wait_recv()
            mate_ring.forward()

        @pl.when(p == 4)
        def _():
            mate_ring.up[1].wait_recv()

        @pl.when(p == 5)
        def _():
            mate_ring.down[0].wait_recv()
            proj_ring.forward()

        @pl.when(p == 6)
        def _():
            own_ring.far()

        @pl.when(p == 7)
        def _():
            mate_ring.far()

        step = jnp.where(p < 2, 0, jnp.where(p >= 6, 2, jnp.where(lax.rem(p, 2) == 0, 3, 1)))
        is_own = (p == 0) | (p == 2) | (p == 3) | (p == 6)
        zo = around(z, step)
        yo = jnp.where(is_own, yh, mate)

        @pl.loop(0, 4)
        def _(i):
            s = around(x, jnp.where(i == 0, 2, jnp.where(i == 1, 1, jnp.where(i == 2, 3, 0))))
            work(s, zo, yo)

            @pl.when(p == 7)
            def _():
                lane = lax.broadcasted_iota(jnp.int32, (32, 128), 1)
                for c in range(2):
                    t = jnp.zeros((32, 128), F32)
                    for j in range(8):
                        rows = slice(j * 32, (j + 1) * 32)
                        t = jnp.where(lane == j, m_s[s, c, rows, :], t)
                        t = jnp.where(lane == 8 + j, l_s[s, c, rows, :], t)
                    part_stat[s, c] = t

                @pl.when(s != x)
                def _():
                    acc_copy(s).start()
                    stat_copy(s).start()

                @pl.when(s == x)
                def _():
                    pltpu.make_async_copy(acc.at[s], racc.at[x], r_s.at[part_at + x]).start()
                    pltpu.make_async_copy(part_stat.at[s], rstat.at[x], r_s.at[part_at + 4 + x]).start()

    lex_copy.start()
    for i in range(4):
        remote(part_stat.at[i], rstat.at[i], s_s.at[part_at + 4 + i], r_s.at[part_at + 4 + i],
               at_x(around(x, 1))).wait_recv()
        remote(acc.at[i], racc.at[i], s_s.at[part_at + i], r_s.at[part_at + i],
               at_x(around(x, 1))).wait_recv()

    for c in range(2):
        tops = [rstat[i, c] for i in range(4)]
        sums = [pltpu.roll(t, 120, 1) for t in tops]
        top = jnp.maximum(jnp.maximum(tops[0], tops[1]), jnp.maximum(tops[2], tops[3]))
        shares = [jnp.exp2((t - top) * EXP2_SCALE) for t in tops]
        den = sum(a * b for a, b in zip(shares, sums))
        joined_rows = []
        for j in range(8):
            rows = slice(j * 32, (j + 1) * 32)
            num = sum(shares[i][:, j : j + 1] * racc[i, c, rows, :] for i in range(4))
            joined_rows.append((num / den[:, j : j + 1]).astype(BF16))
        rows_all[z, c * 32 : (c + 1) * 32, pl.ds(pl.multiple_of(yh * 1024, 1024), 1024)] = (
            jnp.concatenate(joined_rows, axis=1)
        )
    for i in range(4):
        @pl.when(i != x)
        def _():
            acc_copy(i).wait_send()
            stat_copy(i).wait_send()
    for i in range(2):
        @pl.when(jnp.logical_not(diagonal & (i == yh)))
        def _():
            q_send(i).wait_send()

    def rows_at(o, yo, h):
        return rows_all.at[o, :, pl.ds(pl.multiple_of(yo * 1024 + h * 512, 512), 512)]

    own_cols = pl.ds(pl.multiple_of(yh * 1024, 1024), 1024)
    pair = single(rows_all.at[z, :, own_cols], rows_all.at[z, :, own_cols], {"ctx_2": mate})
    pair.start()
    own_rows = ring(lambda o, h: rows_at(o, yh, h), at_z, z)
    mate_rows = ring(lambda o, h: rows_at(o, mate, h), at_z, z)
    own_rows.start()
    pair.wait_recv()
    mate_rows.start()
    own_rows.forward()
    mate_rows.forward()
    for r in (own_rows, mate_rows):
        r.near()
        r.far()
    proj_ring.near()
    proj_ring.far()

    def project(a, b):
        return jnp.dot(
            rows_all[...].reshape(256, 2048), proj[2 * a + b], preferred_element_type=F32
        )

    crossings = []
    for q in range(2):
        mixed[q, other] = project(q, other)
        c = single(mixed.at[q, other], from_core.at[q], at_core(other))
        c.start()
        crossings.append(c)
    for q in range(2):
        mixed[q, core] = project(q, core)
    for q, c in enumerate(crossings):
        c.wait_recv()
        from_core[q] = mixed[q, core] + from_core[q]
    c = single(from_core.at[1 - yl], from_y, {"head_0": 1 - yl})
    c.start()
    from_twin(skip_ref, skip, skip_at)
    from_twin(gain_ref, gain, skip_at + 1)
    c.wait_recv()
    hidden = (skip[...].astype(F32) + (from_core[yl] + from_y[...])).astype(BF16)
    back[0] = hidden
    back_at = take(1)
    to_twin(back.at[0], back.at[1], back_at)
    wide = hidden.astype(F32)

    part = jnp.sum(jnp.transpose(wide * wide), axis=0, keepdims=True)
    sq_c[core] = jnp.broadcast_to(part, (8, 256))
    c = single(sq_c.at[core], sq_c.at[core], at_core(other))
    c.start()
    c.wait_recv()
    sq[z, y] = sq_c[0] + sq_c[1]
    shared = []
    for d in range(4):
        for e in range(4):
            if d or e:
                peer = {**at_z(around(z, d)), **at_y(around(y, e))}
                c = single(sq.at[z, y], sq.at[z, y], peer)
                c.start()
                shared.append(c)
    for c in shared:
        c.wait_recv()
    part = sum(sq[i // 4, i % 4, 0:1] for i in range(16))
    factor = jnp.transpose(jnp.broadcast_to(lax.rsqrt(part / D + EPS), (256, 256)))
    norm[z, x, y, core] = (wide * factor * gain[...]).astype(BF16)

    r0, r1, r2 = pl.ds(0, 96), pl.ds(96, 80), pl.ds(176, 80)

    def cols(h):
        return pl.ds(h * 128, 128)

    run_rings([
        ring(lambda o, h: norm.at[o, x, y, core, r0, cols(h)], at_z, z),
        ring(lambda o, h: norm.at[z, o, y, core, r1, cols(h)], at_x, x),
        ring(lambda o, h: norm.at[z, x, o, core, r2, cols(h)], at_y, y),
    ])
    run_rings([
        ring(lambda o, h: norm.at[:, o, y, core, r0, cols(h)], at_x, x),
        ring(lambda o, h: norm.at[z, :, o, core, r1, cols(h)], at_y, y),
        ring(lambda o, h: norm.at[o, x, :, core, r2, cols(h)], at_z, z),
    ])
    last = [
        ring(lambda o, h: norm.at[:, :, o, core, r0, cols(h)], at_y, y),
        ring(lambda o, h: norm.at[o, :, :, core, r1, cols(h)], at_z, z),
        ring(lambda o, h: norm.at[:, o, :, core, r2, cols(h)], at_x, x),
    ]
    parts = [
        lambda o: norm.at[:, :, o, core, r0],
        lambda o: norm.at[o, :, :, core, r1],
        lambda o: norm.at[:, o, :, core, r2],
    ]
    arrivals = []

    def hand_over(ref):
        c = single(ref, ref, at_core(other))
        c.start()
        arrivals.append(c)

    for r in last:
        r.start()
    for f, own in zip(parts, (y, z, x)):
        hand_over(f(own))
    for r in last:
        r.forward()
    for r, f in zip(last, parts):
        r.near()
        hand_over(f(r.plus))
        hand_over(f(r.minus))
    for r, f in zip(last, parts):
        r.far()
        hand_over(f(r.opp))
    lex_copy.wait()

    def add(cc, fresh):
        for zz in range(4):
            first = zz * 2048 + cc * 512
            b = jnp.concatenate(
                [lex[pl.ds(pl.multiple_of(first + i * 1024, 512), 512), :] for i in range(2)], axis=0
            )
            for g in range(0, 4, GROUPS):
                a = jnp.concatenate([
                    jnp.concatenate([norm[zz, q, yy, cc] for yy in (0, 2, 1, 3)], axis=1)
                    for q in range(g, g + GROUPS)
                ], axis=0)
                t = jnp.dot(a, b, preferred_element_type=F32)
                rows = slice(g * 256, (g + GROUPS) * 256)
                if fresh and zz == 0:
                    logit[rows, :] = t
                else:
                    logit[rows, :] += t

    add(core, True)
    for c in arrivals:
        c.wait_recv()
    add(other, False)

    offset = (((z * 4 + x) * 2 + yh) * 4 + yl * 2 + core) * 512
    for group in range(4):
        rows = slice(group * 256, (group + 1) * 256)
        logits = logit[rows, :] / column(div_ref[:, rows])
        ids = lax.broadcasted_iota(jnp.int32, logits.shape, 1) + offset
        picked = jnp.sum(jnp.where(ids == column(tok_ref[:, rows]), logits, 0.0), axis=1, keepdims=True)
        peak = jnp.max(logits, axis=1, keepdims=True)
        total = jnp.sum(jnp.exp(logits - peak), axis=1, keepdims=True)
        lane = lax.broadcasted_iota(jnp.int32, (256, 128), 1)
        both = jnp.where(lane == 0, peak, jnp.where(lane == 1, total, picked))
        stat[0, z, :, rows] = jnp.transpose(both)[0:8, :]

    def joined(tiles):
        peak = tiles[0][0:1]
        for t in tiles[1:]:
            peak = jnp.maximum(peak, t[0:1])
        total = sum(t[1:2] * jnp.exp(t[0:1] - peak) for t in tiles)
        picked = sum(t[2:3] for t in tiles)
        return peak, total, picked

    def spread(values):
        sub = lax.broadcasted_iota(jnp.int32, (8, 1024), 0)
        return jnp.where(sub == 0, values[0], jnp.where(sub == 1, values[1], values[2]))

    values = None
    for stage, (dev, me) in enumerate(((at_z, z), (at_x, x), (at_y, y))):
        if stage:
            stat[stage, me] = spread(values)
        swap(stat.at[stage], dev, me)
        values = joined([stat[stage, i] for i in range(4)])
    stat_c[core] = spread(values)
    c = single(stat_c.at[core], stat_c.at[core], at_core(other))
    c.start()
    c.wait_recv()
    peak, total, picked = joined([stat_c[0], stat_c[1]])
    logprob_ref[...] = picked - peak - jnp.log(total)

    from_twin(back.at[0], back.at[1], back_at)
    hidden_ref[...] = back[1]
    twin_sent(skip_ref, skip, skip_at)
    twin_sent(gain_ref, gain, skip_at + 1)
    twin_sent(back.at[0], back.at[1], back_at)
    for wait in pending:
        wait()


def whole(q, k, v, loc, proj, skip, gain, lex, div, tok):
    vmem = pl.BlockSpec(memory_space=pltpu.VMEM)
    hbm = pl.BlockSpec(memory_space=pl.ANY)
    return pl.pallas_call(
        kernel,
        out_shape=(
            jax.ShapeDtypeStruct((256, 256), BF16),
            jax.ShapeDtypeStruct((1, 1024), F32),
        ),
        in_specs=[hbm, hbm, hbm, vmem, hbm, vmem, vmem, hbm, vmem, vmem],
        out_specs=(vmem, vmem),
        scratch_shapes=[
            pltpu.VMEM((4, 64, 1024), BF16),
            pltpu.VMEM((4, 2, 1024, 128), BF16),
            pltpu.VMEM((4, 2, 1024, 128), BF16),
            pltpu.VMEM((1024, 128), jnp.int32),
            pltpu.VMEM((4, 2, 256, 1), F32),
            pltpu.VMEM((4, 2, 256, 1), F32),
            pltpu.VMEM((4, 2, 256, 128), F32),
            pltpu.VMEM((4, 2, 32, 128), F32),
            pltpu.VMEM((4, 2, 256, 128), F32),
            pltpu.VMEM((4, 2, 32, 128), F32),
            pltpu.VMEM((4, 64, 2048), BF16),
            pltpu.VMEM((4, 2048, 256), BF16),
            pltpu.VMEM((2, 2, 256, 256), F32),
            pltpu.VMEM((2, 256, 256), F32),
            pltpu.VMEM((256, 256), F32),
            pltpu.VMEM((256, 256), BF16),
            pltpu.VMEM((1, 256), F32),
            pltpu.VMEM((2, 256, 256), BF16),
            pltpu.VMEM((2, 8, 256), F32),
            pltpu.VMEM((4, 4, 8, 256), F32),
            pltpu.VMEM((4, 4, 4, 2, 256, 256), BF16),
            pltpu.VMEM((8192, 512), BF16),
            pltpu.VMEM((1024, 512), F32),
            pltpu.VMEM((3, 4, 8, 1024), F32),
            pltpu.VMEM((2, 8, 1024), F32),
            pltpu.SemaphoreType.DMA((4,)),
            pltpu.SemaphoreType.DMA((192,)),
            pltpu.SemaphoreType.DMA((192,)),
        ],
        compiler_params=pltpu.CompilerParams(
            collective_id=0, has_side_effects=True, vmem_limit_bytes=58 * 1024 * 1024
        ),
        name="whole",
    )(q, k, v, loc, proj, skip, gain, lex, div, tok)


def shards(q, k, v, loc, proj, skip, gain, lex, div, tok):
    hidden, logprob = whole(
        q, k, v, loc.reshape(1, 1024), proj, skip, gain.reshape(1, 256), lex,
        div.reshape(1, 1024), tok.reshape(1, 1024)
    )
    return hidden, logprob.reshape(1024)


def solution(mesh):
    torus = Mesh(mesh.devices.reshape(4, 4, 2, 2, 2), CTX_HEAD)
    placed = (
        P(CTX, HEAD),
        P(CTX, HEAD),
        P(CTX, HEAD),
        P(),
        P(HEAD, CTX),
        P(HEAD, CTX),
        P(CTX),
        P(None, CTX_HEAD),
        P(),
        P(),
    )
    return jax.shard_map(
        shards, mesh=torus, in_specs=placed, out_specs=(P(HEAD, CTX), P()), check_vma=False
    )
```

```python
import jax
import jax.numpy as jnp
from jax import lax
from jax.experimental import pallas as pl
from jax.experimental.pallas import tpu as pltpu
from jax.sharding import Mesh
from jax.sharding import PartitionSpec as P

D = 8192
EPS = 1e-05
LOW = -1e30
GROUPS = 2
LOG2E = 1.4426950408889634
EXP2_SCALE = 128 ** (-0.5) * LOG2E
CTX = ("ctx_0", "ctx_1", "ctx_2")
HEAD = ("head_0", "head_1")
CTX_HEAD = CTX + HEAD
F32 = jnp.float32
BF16 = jnp.bfloat16
MESH = pl.DeviceIdType.MESH


def at_z(p):
    return {"ctx_0": p}


def at_x(p):
    return {"ctx_1": p}


def at_y(p):
    return {"ctx_2": lax.div(p, 2), "head_0": lax.rem(p, 2)}


def at_core(p):
    return {"head_1": p}


def around(p, d):
    return lax.rem(p + d, 4)


def remote(src, dst, ssem, rsem, dev):
    return pltpu.make_async_remote_copy(
        src_ref=src, dst_ref=dst, send_sem=ssem, recv_sem=rsem, device_id=dev, device_id_type=MESH
    )


def greet(dev):
    pl.semaphore_signal(pltpu.get_barrier_semaphore(), inc=1, device_id=dev, device_id_type=MESH)


class Ring:
    def __init__(self, piece, ssem, rsem, base, dev, me):
        self.piece, self.ssem, self.rsem, self.base, self.dev = piece, ssem, rsem, base, dev
        self.plus, self.minus, self.opp = around(me, 1), around(me, 3), around(me, 2)
        self.up = [self.copy(me, h, h, self.plus) for h in range(2)]
        self.down = [self.copy(me, h, 2 + h, self.minus) for h in range(2)]
        self.on_up = self.copy(self.minus, 0, 4, self.plus)
        self.on_down = self.copy(self.plus, 1, 5, self.minus)

    def copy(self, origin, half, n, peer):
        ref = self.piece(origin, half)
        return remote(ref, ref, self.ssem.at[self.base + n], self.rsem.at[self.base + n], self.dev(peer))

    def start(self):
        self.up[0].start()
        self.down[1].start()
        self.up[1].start()
        self.down[0].start()

    def forward(self):
        self.up[0].wait_recv()
        self.on_up.start()
        self.down[1].wait_recv()
        self.on_down.start()

    def near(self):
        self.up[1].wait_recv()
        self.down[0].wait_recv()

    def far(self):
        self.on_up.wait_recv()
        self.on_down.wait_recv()

    def sent(self):
        for c in (*self.up, *self.down, self.on_up, self.on_down):
            c.wait_send()


def run_rings(rings):
    for r in rings:
        r.start()
    for r in rings:
        r.forward()
    for r in rings:
        r.near()
    for r in rings:
        r.far()


class Swap:
    def __init__(self, buf, ssem, rsem, base, dev, me):
        self.copies = [
            remote(buf.at[me], buf.at[me], ssem.at[base + d], rsem.at[base + d], dev(around(me, d)))
            for d in (1, 2, 3)
        ]

    def run(self):
        for c in self.copies:
            c.start()
        for c in self.copies:
            c.wait_recv()

    def sent(self):
        for c in self.copies:
            c.wait_send()


def column(row):
    return jnp.transpose(jnp.broadcast_to(row, (128, row.shape[1])))[:, 0:1]


def kernel(
    q_hbm, k_hbm, v_hbm, loc_hbm, proj_hbm, skip_ref, gain_ref, lex_hbm, div_hbm, tok_hbm,
    hidden_ref, logprob_ref,
    loc_ref, div_ref, tok_ref,
    qbuf, kbuf, vbuf, loc_col, m_s, l_s, acc, part_stat, racc, rstat,
    rows_all, proj, mixed, from_core, from_y, skip, gain, back, sq_c, sq, norm, lex, logit, stat, stat_c,
    l_sem, s_s, r_s,
):
    z, x, yh = lax.axis_index("ctx_0"), lax.axis_index("ctx_1"), lax.axis_index("ctx_2")
    yl, core = lax.axis_index("head_0"), lax.axis_index("head_1")
    y = 2 * yh + yl
    other, mate = 1 - core, 1 - yh
    diagonal = x == z
    head = 2 * yl + core
    twin = {"ctx_1": head, "head_0": lax.div(x, 2), "head_1": lax.rem(x, 2)}
    is_twin = x == head

    proj_copy = pltpu.make_async_copy(proj_hbm, proj.at[x], l_sem.at[0])
    lex_copy = pltpu.make_async_copy(lex_hbm, lex, l_sem.at[1])

    def head_cols(ref, g):
        return ref.at[:, pl.ds(pl.multiple_of(g * 128, 128), 128)]

    own_k = pltpu.make_async_copy(head_cols(k_hbm, yh), kbuf.at[z, yh], l_sem.at[2])
    own_v = pltpu.make_async_copy(head_cols(v_hbm, yh), vbuf.at[z, yh], l_sem.at[3])
    small = [
        pltpu.make_async_copy(a, b, l_sem.at[4 + i])
        for i, (a, b) in enumerate(((loc_hbm, loc_ref), (div_hbm, div_ref), (tok_hbm, tok_ref)))
    ]
    own_k.start()
    own_v.start()
    proj_copy.start()
    for c in small:
        c.start()

    for d in (1, 2, 3):
        greet(at_z(around(z, d)))
        greet(at_x(around(x, d)))
        greet(at_y(around(y, d)))
        for e in (1, 2, 3):
            greet({**at_z(around(z, d)), **at_y(around(y, e))})
    greet(at_core(other))
    for i in range(2):
        @pl.when(jnp.logical_not(diagonal & (i == yh)))
        def _():
            greet({"ctx_0": x, "ctx_1": z, "ctx_2": i})
    @pl.when(jnp.logical_not(is_twin))
    def _():
        greet(twin)
    pl.semaphore_wait(
        pltpu.get_barrier_semaphore(), 19 + jnp.where(diagonal, 1, 2) + jnp.where(is_twin, 0, 1)
    )

    pending = []
    count = [0]

    def take(n):
        count[0] += n
        return count[0] - n

    def ring(piece, dev, me):
        r = Ring(piece, s_s, r_s, take(6), dev, me)
        pending.append(r.sent)
        return r

    def single(src, dst, dev):
        n = take(1)
        c = remote(src, dst, s_s.at[n], r_s.at[n], dev)
        pending.append(c.wait_send)
        return c

    def swap(buf, dev, me):
        s = Swap(buf, s_s, r_s, take(4), dev, me)
        pending.append(s.sent)
        s.run()

    def to_twin(src, dst, n):
        @pl.when(is_twin)
        def _():
            pltpu.make_async_copy(src, dst, r_s.at[n]).start()
        @pl.when(jnp.logical_not(is_twin))
        def _():
            remote(src, dst, s_s.at[n], r_s.at[n], twin).start()

    def from_twin(src, dst, n):
        remote(src, dst, s_s.at[n], r_s.at[n], twin).wait_recv()

    def twin_sent(src, dst, n):
        @pl.when(jnp.logical_not(is_twin))
        def _():
            remote(src, dst, s_s.at[n], r_s.at[n], twin).wait_send()

    q_at = take(2)

    def q_copies(i):
        src = q_hbm.at[:, i * 1024 : (i + 1) * 1024]
        dst = qbuf.at[z, pl.ds(pl.multiple_of(yh * 32, 32), 32)]
        return src, dst

    def q_send(i):
        peer = {"ctx_0": x, "ctx_1": z, "ctx_2": i}
        return remote(*q_copies(i), s_s.at[q_at + i], r_s.at[q_at + yh], peer)

    for i in range(2):
        to_self = diagonal & (i == yh)
        @pl.when(jnp.logical_not(to_self))
        def _():
            q_send(i).start()
        @pl.when(to_self)
        def _():
            pltpu.make_async_copy(*q_copies(i), r_s.at[q_at + yh]).start()

    k_swap = single(head_cols(k_hbm, mate), kbuf.at[z, yh], {"ctx_2": mate})
    v_swap = single(head_cols(v_hbm, mate), vbuf.at[z, yh], {"ctx_2": mate})
    k_swap.start()
    v_swap.start()

    def kv_ring(yo):
        return ring(lambda o, h: (vbuf if h else kbuf).at[o, yo], at_z, z)

    own_ring, mate_ring = kv_ring(yh), kv_ring(mate)
    own_k.wait()
    own_v.wait()
    own_ring.start()

    m_s[...] = jnp.full(m_s.shape, LOW, F32)
    l_s[...] = jnp.zeros(l_s.shape, F32)
    acc[...] = jnp.zeros(acc.shape, F32)
    for c in small:
        c.wait()
    for i in range(8):
        cols = slice(i * 128, (i + 1) * 128)
        loc_col[cols, :] = jnp.transpose(jnp.broadcast_to(loc_ref[:, cols], (128, 128)))

    for i in range(2):
        dst = qbuf.at[x, i * 32 : (i + 1) * 32]
        remote(dst, dst, s_s.at[q_at], r_s.at[q_at + i], at_x(around(x, 1))).wait_recv()
    q_ring = ring(lambda o, h: qbuf.at[o, :, h * 512 : (h + 1) * 512], at_x, x)
    q_ring.start()
    own_ring.forward()
    q_ring.forward()

    proj_copy.wait()
    proj_ring = ring(lambda o, h: proj.at[o, h * 1024 : (h + 1) * 1024], at_x, x)
    proj_ring.start()

    k_swap.wait_recv()
    v_swap.wait_recv()
    mate_ring.start()
    q_ring.near()
    q_ring.far()

    skip_at = take(2)
    to_twin(skip_ref, skip, skip_at)
    to_twin(gain_ref, gain, skip_at + 1)

    def tile(s, c, zo, yo, masked):
        q = jnp.concatenate(
            [qbuf[s, c * 32 : (c + 1) * 32, j * 128 : (j + 1) * 128] for j in range(8)], axis=0
        )
        raw = lax.dot_general(
            q, kbuf[zo, yo], (((1,), (1,)), ((), ())), preferred_element_type=F32
        )
        if masked:
            base = 8 * zo + 2 * x + yo
            first = pl.multiple_of(base * 32, 32)
            loc = loc_col[pl.ds(first, 32), 0:1] - base * 1024
            loc = jnp.concatenate([loc] * 8, axis=0)
            pos = lax.broadcasted_iota(jnp.int32, raw.shape, 1)
            raw = jnp.where(pos <= loc, raw, LOW)
        top = jnp.max(raw, axis=1, keepdims=True)
        w = jnp.exp2((raw - top) * EXP2_SCALE)
        total = jnp.sum(w, axis=1, keepdims=True)
        part = jnp.dot(w.astype(BF16), vbuf[zo, yo], preferred_element_type=F32)
        m_old = m_s[s, c]
        m_new = jnp.maximum(m_old, top)
        a = jnp.exp2((m_old - m_new) * EXP2_SCALE)
        b = jnp.exp2((top - m_new) * EXP2_SCALE)
        m_s[s, c] = m_new
        l_s[s, c] = l_s[s, c] * a + total * b
        acc[s, c] = acc[s, c] * a + part * b

    def work(s, zo, yo):
        chunk = 8 * s + 2 * z
        block = 8 * zo + 2 * x + yo

        @pl.when(chunk > block)
        def _():
            tile(s, 0, zo, yo, False)
            tile(s, 1, zo, yo, False)

        @pl.when(chunk == block)
        def _():
            tile(s, 0, zo, yo, True)
            tile(s, 1, zo, yo, False)

        @pl.when(chunk + 1 == block)
        def _():
            tile(s, 1, zo, yo, True)

    part_at = take(8)

    def acc_copy(s):
        return remote(acc.at[s], racc.at[x], s_s.at[part_at + s], r_s.at[part_at + x], at_x(s))

    def stat_copy(s):
        return remote(part_stat.at[s], rstat.at[x], s_s.at[part_at + 4 + s],
                      r_s.at[part_at + 4 + x], at_x(s))

    @pl.loop(0, 8)
    def _(p):
        @pl.when(p == 2)
        def _():
            own_ring.up[1].wait_recv()

        @pl.when(p == 3)
        def _():
            own_ring.down[0].wait_recv()
            mate_ring.forward()

        @pl.when(p == 4)
        def _():
            mate_ring.up[1].wait_recv()

        @pl.when(p == 5)
        def _():
            mate_ring.down[0].wait_recv()
            proj_ring.forward()

        @pl.when(p == 6)
        def _():
            own_ring.far()

        @pl.when(p == 7)
        def _():
            mate_ring.far()

        step = jnp.where(p < 2, 0, jnp.where(p >= 6, 2, jnp.where(lax.rem(p, 2) == 0, 3, 1)))
        is_own = (p == 0) | (p == 2) | (p == 3) | (p == 6)
        zo = around(z, step)
        yo = jnp.where(is_own, yh, mate)

        @pl.loop(0, 4)
        def _(i):
            s = around(x, jnp.where(i == 0, 2, jnp.where(i == 1, 1, jnp.where(i == 2, 3, 0))))
            work(s, zo, yo)

            @pl.when(p == 7)
            def _():
                lane = lax.broadcasted_iota(jnp.int32, (32, 128), 1)
                for c in range(2):
                    t = jnp.zeros((32, 128), F32)
                    for j in range(8):
                        rows = slice(j * 32, (j + 1) * 32)
                        t = jnp.where(lane == j, m_s[s, c, rows, :], t)
                        t = jnp.where(lane == 8 + j, l_s[s, c, rows, :], t)
                    part_stat[s, c] = t

                @pl.when(s != x)
                def _():
                    acc_copy(s).start()
                    stat_copy(s).start()

                @pl.when(s == x)
                def _():
                    pltpu.make_async_copy(acc.at[s], racc.at[x], r_s.at[part_at + x]).start()
                    pltpu.make_async_copy(part_stat.at[s], rstat.at[x], r_s.at[part_at + 4 + x]).start()

    lex_copy.start()
    for i in range(4):
        remote(part_stat.at[i], rstat.at[i], s_s.at[part_at + 4 + i], r_s.at[part_at + 4 + i],
               at_x(around(x, 1))).wait_recv()
        remote(acc.at[i], racc.at[i], s_s.at[part_at + i], r_s.at[part_at + i],
               at_x(around(x, 1))).wait_recv()

    for c in range(2):
        tops = [rstat[i, c] for i in range(4)]
        sums = [pltpu.roll(t, 120, 1) for t in tops]
        top = jnp.maximum(jnp.maximum(tops[0], tops[1]), jnp.maximum(tops[2], tops[3]))
        shares = [jnp.exp2((t - top) * EXP2_SCALE) for t in tops]
        den = sum(a * b for a, b in zip(shares, sums))
        joined_rows = []
        for j in range(8):
            rows = slice(j * 32, (j + 1) * 32)
            num = sum(shares[i][:, j : j + 1] * racc[i, c, rows, :] for i in range(4))
            joined_rows.append((num / den[:, j : j + 1]).astype(BF16))
        rows_all[z, c * 32 : (c + 1) * 32, pl.ds(pl.multiple_of(yh * 1024, 1024), 1024)] = (
            jnp.concatenate(joined_rows, axis=1)
        )
    for i in range(4):
        @pl.when(i != x)
        def _():
            acc_copy(i).wait_send()
            stat_copy(i).wait_send()
    for i in range(2):
        @pl.when(jnp.logical_not(diagonal & (i == yh)))
        def _():
            q_send(i).wait_send()

    def rows_at(o, yo, h):
        return rows_all.at[o, :, pl.ds(pl.multiple_of(yo * 1024 + h * 512, 512), 512)]

    own_cols = pl.ds(pl.multiple_of(yh * 1024, 1024), 1024)
    pair = single(rows_all.at[z, :, own_cols], rows_all.at[z, :, own_cols], {"ctx_2": mate})
    pair.start()
    own_rows = ring(lambda o, h: rows_at(o, yh, h), at_z, z)
    mate_rows = ring(lambda o, h: rows_at(o, mate, h), at_z, z)
    own_rows.start()
    pair.wait_recv()
    mate_rows.start()
    own_rows.forward()
    mate_rows.forward()
    for r in (own_rows, mate_rows):
        r.near()
        r.far()
    proj_ring.near()
    proj_ring.far()

    def project(a, b):
        return jnp.dot(
            rows_all[...].reshape(256, 2048), proj[2 * a + b], preferred_element_type=F32
        )

    cross_at = take(2)
    away = 1 - yl
    mixed[away, other] = project(away, other)
    crossing_away = remote(
        mixed.at[away, other], from_core.at[away], s_s.at[cross_at], r_s.at[cross_at + away], at_core(other)
    )
    crossing_away.start()
    mixed[away, core] = project(away, core)
    mixed[yl, other] = project(yl, other)
    crossing_home = remote(
        mixed.at[yl, other], from_core.at[yl], s_s.at[cross_at + 1], r_s.at[cross_at + yl], at_core(other)
    )
    crossing_home.start()
    crossing_away.wait_recv()
    from_core[away] = mixed[away, core] + from_core[away]
    c = single(from_core.at[away], from_y, {"head_0": away})
    c.start()
    mixed[yl, core] = project(yl, core)
    crossing_home.wait_recv()
    from_core[yl] = mixed[yl, core] + from_core[yl]
    pending.append(crossing_away.wait_send)
    pending.append(crossing_home.wait_send)
    from_twin(skip_ref, skip, skip_at)
    from_twin(gain_ref, gain, skip_at + 1)
    c.wait_recv()
    hidden = (skip[...].astype(F32) + (from_core[yl] + from_y[...])).astype(BF16)
    back[0] = hidden
    back_at = take(1)
    to_twin(back.at[0], back.at[1], back_at)
    wide = hidden.astype(F32)

    part = jnp.sum(jnp.transpose(wide * wide), axis=0, keepdims=True)
    sq_c[core] = jnp.broadcast_to(part, (8, 256))
    c = single(sq_c.at[core], sq_c.at[core], at_core(other))
    c.start()
    c.wait_recv()
    sq[z, y] = sq_c[0] + sq_c[1]
    shared = []
    for d in range(4):
        for e in range(4):
            if d or e:
                peer = {**at_z(around(z, d)), **at_y(around(y, e))}
                c = single(sq.at[z, y], sq.at[z, y], peer)
                c.start()
                shared.append(c)
    for c in shared:
        c.wait_recv()
    part = sum(sq[i // 4, i % 4, 0:1] for i in range(16))
    factor = jnp.transpose(jnp.broadcast_to(lax.rsqrt(part / D + EPS), (256, 256)))
    norm[z, x, y, core] = (wide * factor * gain[...]).astype(BF16)

    r0, r1, r2 = pl.ds(0, 96), pl.ds(96, 80), pl.ds(176, 80)

    def cols(h):
        return pl.ds(h * 128, 128)

    own = norm.at[z, x, y, core]
    near = []
    for d in (2, 1, 3):
        for rows, dev, me in ((r0, at_z, z), (r1, at_x, x), (r2, at_y, y)):
            c = single(own.at[rows], own.at[rows], dev(around(me, d)))
            c.start()
            near.append(c)
    for c in near:
        c.wait_recv()
    run_rings([
        ring(lambda o, h: norm.at[:, o, y, core, r0, cols(h)], at_x, x),
        ring(lambda o, h: norm.at[z, :, o, core, r1, cols(h)], at_y, y),
        ring(lambda o, h: norm.at[o, x, :, core, r2, cols(h)], at_z, z),
    ])
    earlier = list(pending)
    pending.clear()
    last = [
        ring(lambda o, h: norm.at[:, :, o, core, r0, cols(h)], at_y, y),
        ring(lambda o, h: norm.at[o, :, :, core, r1, cols(h)], at_z, z),
        ring(lambda o, h: norm.at[:, o, :, core, r2, cols(h)], at_x, x),
    ]
    parts = [
        lambda o: norm.at[:, :, o, core, r0],
        lambda o: norm.at[o, :, :, core, r1],
        lambda o: norm.at[:, o, :, core, r2],
    ]
    arrivals = []

    def hand_over(ref):
        c = single(ref, ref, at_core(other))
        c.start()
        arrivals.append(c)

    for r in last:
        r.start()
    for f, own in zip(parts, (y, z, x)):
        hand_over(f(own))
    for r in last:
        r.forward()
    for wait in earlier:
        wait()
    twin_sent(skip_ref, skip, skip_at)
    twin_sent(gain_ref, gain, skip_at + 1)
    for r, f in zip(last, parts):
        r.near()
        hand_over(f(r.plus))
        hand_over(f(r.minus))
    for r, f in zip(last, parts):
        r.far()
        hand_over(f(r.opp))
    lex_copy.wait()

    def add(cc, fresh):
        for zz in range(4):
            first = zz * 2048 + cc * 512
            b = jnp.concatenate(
                [lex[pl.ds(pl.multiple_of(first + i * 1024, 512), 512), :] for i in range(2)], axis=0
            )
            for g in range(0, 4, GROUPS):
                a = jnp.concatenate([
                    jnp.concatenate([norm[zz, q, yy, cc] for yy in (0, 2, 1, 3)], axis=1)
                    for q in range(g, g + GROUPS)
                ], axis=0)
                t = jnp.dot(a, b, preferred_element_type=F32)
                rows = slice(g * 256, (g + GROUPS) * 256)
                if fresh and zz == 0:
                    logit[rows, :] = t
                else:
                    logit[rows, :] += t

    add(core, True)
    for c in arrivals:
        c.wait_recv()
    add(other, False)

    offset = (((z * 4 + x) * 2 + yh) * 4 + yl * 2 + core) * 512
    for group in range(4):
        rows = slice(group * 256, (group + 1) * 256)
        logits = logit[rows, :] / column(div_ref[:, rows])
        ids = lax.broadcasted_iota(jnp.int32, logits.shape, 1) + offset
        picked = jnp.sum(jnp.where(ids == column(tok_ref[:, rows]), logits, 0.0), axis=1, keepdims=True)
        peak = jnp.max(logits, axis=1, keepdims=True)
        total = jnp.sum(jnp.exp(logits - peak), axis=1, keepdims=True)
        lane = lax.broadcasted_iota(jnp.int32, (256, 128), 1)
        both = jnp.where(lane == 0, peak, jnp.where(lane == 1, total, picked))
        stat[0, z, :, rows] = jnp.transpose(both)[0:8, :]

    def joined(tiles):
        peak = tiles[0][0:1]
        for t in tiles[1:]:
            peak = jnp.maximum(peak, t[0:1])
        total = sum(t[1:2] * jnp.exp(t[0:1] - peak) for t in tiles)
        picked = sum(t[2:3] for t in tiles)
        return peak, total, picked

    def spread(values):
        sub = lax.broadcasted_iota(jnp.int32, (8, 1024), 0)
        return jnp.where(sub == 0, values[0], jnp.where(sub == 1, values[1], values[2]))

    values = None
    for stage, (dev, me) in enumerate(((at_z, z), (at_x, x), (at_y, y))):
        if stage:
            stat[stage, me] = spread(values)
        swap(stat.at[stage], dev, me)
        values = joined([stat[stage, i] for i in range(4)])
    stat_c[core] = spread(values)
    c = single(stat_c.at[core], stat_c.at[core], at_core(other))
    c.start()
    c.wait_recv()
    peak, total, picked = joined([stat_c[0], stat_c[1]])
    logprob_ref[...] = picked - peak - jnp.log(total)

    from_twin(back.at[0], back.at[1], back_at)
    hidden_ref[...] = back[1]
    twin_sent(back.at[0], back.at[1], back_at)
    for wait in pending:
        wait()


def whole(q, k, v, loc, proj, skip, gain, lex, div, tok):
    vmem = pl.BlockSpec(memory_space=pltpu.VMEM)
    hbm = pl.BlockSpec(memory_space=pl.ANY)
    return pl.pallas_call(
        kernel,
        out_shape=(
            jax.ShapeDtypeStruct((256, 256), BF16),
            jax.ShapeDtypeStruct((1, 1024), F32),
        ),
        in_specs=[hbm] * 10,
        out_specs=(vmem, vmem),
        scratch_shapes=[
            pltpu.VMEM((1, 1024), jnp.int32),
            pltpu.VMEM((1, 1024), F32),
            pltpu.VMEM((1, 1024), jnp.int32),
            pltpu.VMEM((4, 64, 1024), BF16),
            pltpu.VMEM((4, 2, 1024, 128), BF16),
            pltpu.VMEM((4, 2, 1024, 128), BF16),
            pltpu.VMEM((1024, 128), jnp.int32),
            pltpu.VMEM((4, 2, 256, 1), F32),
            pltpu.VMEM((4, 2, 256, 1), F32),
            pltpu.VMEM((4, 2, 256, 128), F32),
            pltpu.VMEM((4, 2, 32, 128), F32),
            pltpu.VMEM((4, 2, 256, 128), F32),
            pltpu.VMEM((4, 2, 32, 128), F32),
            pltpu.VMEM((4, 64, 2048), BF16),
            pltpu.VMEM((4, 2048, 256), BF16),
            pltpu.VMEM((2, 2, 256, 256), F32),
            pltpu.VMEM((2, 256, 256), F32),
            pltpu.VMEM((256, 256), F32),
            pltpu.VMEM((256, 256), BF16),
            pltpu.VMEM((1, 256), F32),
            pltpu.VMEM((2, 256, 256), BF16),
            pltpu.VMEM((2, 8, 256), F32),
            pltpu.VMEM((4, 4, 8, 256), F32),
            pltpu.VMEM((4, 4, 4, 2, 256, 256), BF16),
            pltpu.VMEM((8192, 512), BF16),
            pltpu.VMEM((1024, 512), F32),
            pltpu.VMEM((3, 4, 8, 1024), F32),
            pltpu.VMEM((2, 8, 1024), F32),
            pltpu.SemaphoreType.DMA((7,)),
            pltpu.SemaphoreType.DMA((192,)),
            pltpu.SemaphoreType.DMA((192,)),
        ],
        compiler_params=pltpu.CompilerParams(
            collective_id=0, has_side_effects=True, vmem_limit_bytes=58 * 1024 * 1024
        ),
        name="whole",
    )(q, k, v, loc, proj, skip, gain, lex, div, tok)


def shards(q, k, v, loc, proj, skip, gain, lex, div, tok):
    hidden, logprob = whole(
        q, k, v, loc.reshape(1, 1024), proj, skip, gain.reshape(1, 256), lex,
        div.reshape(1, 1024), tok.reshape(1, 1024)
    )
    return hidden, logprob.reshape(1024)


def solution(mesh):
    torus = Mesh(mesh.devices.reshape(4, 4, 2, 2, 2), CTX_HEAD)
    placed = (
        P(CTX, HEAD),
        P(CTX, HEAD),
        P(CTX, HEAD),
        P(),
        P(HEAD, CTX),
        P(HEAD, CTX),
        P(CTX),
        P(None, CTX_HEAD),
        P(),
        P(),
    )
    return jax.shard_map(
        shards, mesh=torus, in_specs=placed, out_specs=(P(HEAD, CTX), P()), check_vma=False
    )
```

```python
import jax
import jax.numpy as jnp
from jax import lax
from jax.experimental import pallas as pl
from jax.experimental.pallas import tpu as pltpu
from jax.sharding import Mesh
from jax.sharding import PartitionSpec as P

D = 8192
EPS = 1e-05
LOW = -1e30
GROUPS = 2
LOG2E = 1.4426950408889634
EXP2_SCALE = 128 ** (-0.5) * LOG2E
CTX = ("ctx_0", "ctx_1", "ctx_2")
HEAD = ("head_0", "head_1")
CTX_HEAD = CTX + HEAD
F32 = jnp.float32
BF16 = jnp.bfloat16
MESH = pl.DeviceIdType.MESH


def at_z(p):
    return {"ctx_0": p}


def at_x(p):
    return {"ctx_1": p}


def at_y(p):
    return {"ctx_2": lax.div(p, 2), "head_0": lax.rem(p, 2)}


def at_core(p):
    return {"head_1": p}


def around(p, d):
    return lax.rem(p + d, 4)


def remote(src, dst, ssem, rsem, dev):
    return pltpu.make_async_remote_copy(
        src_ref=src, dst_ref=dst, send_sem=ssem, recv_sem=rsem, device_id=dev, device_id_type=MESH
    )


def greet(dev):
    pl.semaphore_signal(pltpu.get_barrier_semaphore(), inc=1, device_id=dev, device_id_type=MESH)


class Ring:
    def __init__(self, piece, ssem, rsem, base, dev, me):
        self.piece, self.ssem, self.rsem, self.base, self.dev = piece, ssem, rsem, base, dev
        self.plus, self.minus, self.opp = around(me, 1), around(me, 3), around(me, 2)
        self.up = [self.copy(me, h, h, self.plus) for h in range(2)]
        self.down = [self.copy(me, h, 2 + h, self.minus) for h in range(2)]
        self.on_up = self.copy(self.minus, 0, 4, self.plus)
        self.on_down = self.copy(self.plus, 1, 5, self.minus)

    def copy(self, origin, half, n, peer):
        ref = self.piece(origin, half)
        return remote(ref, ref, self.ssem.at[self.base + n], self.rsem.at[self.base + n], self.dev(peer))

    def start(self):
        self.up[0].start()
        self.down[1].start()
        self.up[1].start()
        self.down[0].start()

    def forward(self):
        self.up[0].wait_recv()
        self.on_up.start()
        self.down[1].wait_recv()
        self.on_down.start()

    def near(self):
        self.up[1].wait_recv()
        self.down[0].wait_recv()

    def far(self):
        self.on_up.wait_recv()
        self.on_down.wait_recv()

    def sent(self):
        for c in (*self.up, *self.down, self.on_up, self.on_down):
            c.wait_send()


def run_rings(rings):
    for r in rings:
        r.start()
    for r in rings:
        r.forward()
    for r in rings:
        r.near()
    for r in rings:
        r.far()


class Swap:
    def __init__(self, buf, ssem, rsem, base, dev, me):
        self.copies = [
            remote(buf.at[me], buf.at[me], ssem.at[base + d], rsem.at[base + d], dev(around(me, d)))
            for d in (1, 2, 3)
        ]

    def run(self):
        for c in self.copies:
            c.start()
        for c in self.copies:
            c.wait_recv()

    def sent(self):
        for c in self.copies:
            c.wait_send()


def column(row):
    return jnp.transpose(jnp.broadcast_to(row, (128, row.shape[1])))[:, 0:1]


def kernel(
    q_hbm, k_hbm, v_hbm, loc_hbm, proj_hbm, skip_ref, gain_ref, lex_hbm, div_hbm, tok_hbm,
    hidden_ref, logprob_ref,
    loc_ref, div_ref, tok_ref,
    qbuf, kbuf, vbuf, loc_col, m_s, l_s, acc, part_stat, racc, rstat,
    rows_all, proj, mixed, from_core, from_y, skip, gain, back, sq_c, sq, norm, lex, logit, stat, stat_c,
    l_sem, s_s, r_s,
):
    z, x, yh = lax.axis_index("ctx_0"), lax.axis_index("ctx_1"), lax.axis_index("ctx_2")
    yl, core = lax.axis_index("head_0"), lax.axis_index("head_1")
    y = 2 * yh + yl
    other, mate = 1 - core, 1 - yh
    diagonal = x == z
    head = 2 * yl + core
    twin = {"ctx_1": head, "head_0": lax.div(x, 2), "head_1": lax.rem(x, 2)}
    is_twin = x == head

    proj_copy = pltpu.make_async_copy(proj_hbm, proj.at[x], l_sem.at[0])
    lex_copy = pltpu.make_async_copy(lex_hbm, lex, l_sem.at[1])

    def head_cols(ref, g):
        return ref.at[:, pl.ds(pl.multiple_of(g * 128, 128), 128)]

    own_k = pltpu.make_async_copy(head_cols(k_hbm, yh), kbuf.at[z, yh], l_sem.at[2])
    own_v = pltpu.make_async_copy(head_cols(v_hbm, yh), vbuf.at[z, yh], l_sem.at[3])
    small = [
        pltpu.make_async_copy(a, b, l_sem.at[4 + i])
        for i, (a, b) in enumerate(((loc_hbm, loc_ref), (div_hbm, div_ref), (tok_hbm, tok_ref)))
    ]
    own_k.start()
    own_v.start()
    proj_copy.start()
    for c in small:
        c.start()

    for d in (1, 2, 3):
        greet(at_z(around(z, d)))
        greet(at_x(around(x, d)))
        greet(at_y(around(y, d)))
        for e in (1, 2, 3):
            greet({**at_z(around(z, d)), **at_y(around(y, e))})
    greet(at_core(other))
    for i in range(2):
        @pl.when(jnp.logical_not(diagonal & (i == yh)))
        def _():
            greet({"ctx_0": x, "ctx_1": z, "ctx_2": i})
    @pl.when(jnp.logical_not(is_twin))
    def _():
        greet(twin)
    pl.semaphore_wait(
        pltpu.get_barrier_semaphore(), 19 + jnp.where(diagonal, 1, 2) + jnp.where(is_twin, 0, 1)
    )

    pending = []
    count = [0]

    def take(n):
        count[0] += n
        return count[0] - n

    def ring(piece, dev, me):
        r = Ring(piece, s_s, r_s, take(6), dev, me)
        pending.append(r.sent)
        return r

    def single(src, dst, dev):
        n = take(1)
        c = remote(src, dst, s_s.at[n], r_s.at[n], dev)
        pending.append(c.wait_send)
        return c

    def swap(buf, dev, me):
        s = Swap(buf, s_s, r_s, take(4), dev, me)
        pending.append(s.sent)
        s.run()

    def to_twin(src, dst, n):
        @pl.when(is_twin)
        def _():
            pltpu.make_async_copy(src, dst, r_s.at[n]).start()
        @pl.when(jnp.logical_not(is_twin))
        def _():
            remote(src, dst, s_s.at[n], r_s.at[n], twin).start()

    def from_twin(src, dst, n):
        remote(src, dst, s_s.at[n], r_s.at[n], twin).wait_recv()

    def twin_sent(src, dst, n):
        @pl.when(jnp.logical_not(is_twin))
        def _():
            remote(src, dst, s_s.at[n], r_s.at[n], twin).wait_send()

    q_at = take(2)

    def q_copies(i):
        src = q_hbm.at[:, i * 1024 : (i + 1) * 1024]
        dst = qbuf.at[z, pl.ds(pl.multiple_of(yh * 32, 32), 32)]
        return src, dst

    def q_send(i):
        peer = {"ctx_0": x, "ctx_1": z, "ctx_2": i}
        return remote(*q_copies(i), s_s.at[q_at + i], r_s.at[q_at + yh], peer)

    for i in range(2):
        to_self = diagonal & (i == yh)
        @pl.when(jnp.logical_not(to_self))
        def _():
            q_send(i).start()
        @pl.when(to_self)
        def _():
            pltpu.make_async_copy(*q_copies(i), r_s.at[q_at + yh]).start()

    k_swap = single(head_cols(k_hbm, mate), kbuf.at[z, yh], {"ctx_2": mate})
    v_swap = single(head_cols(v_hbm, mate), vbuf.at[z, yh], {"ctx_2": mate})
    k_swap.start()
    v_swap.start()

    def kv_ring(yo):
        return ring(lambda o, h: (vbuf if h else kbuf).at[o, yo], at_z, z)

    own_ring, mate_ring = kv_ring(yh), kv_ring(mate)
    own_k.wait()
    own_v.wait()
    own_ring.start()

    m_s[...] = jnp.full(m_s.shape, LOW, F32)
    l_s[...] = jnp.zeros(l_s.shape, F32)
    acc[...] = jnp.zeros(acc.shape, F32)
    for c in small:
        c.wait()
    for i in range(8):
        cols = slice(i * 128, (i + 1) * 128)
        loc_col[cols, :] = jnp.transpose(jnp.broadcast_to(loc_ref[:, cols], (128, 128)))

    for i in range(2):
        dst = qbuf.at[x, i * 32 : (i + 1) * 32]
        remote(dst, dst, s_s.at[q_at], r_s.at[q_at + i], at_x(around(x, 1))).wait_recv()
    q_ring = ring(lambda o, h: qbuf.at[o, :, h * 512 : (h + 1) * 512], at_x, x)
    q_ring.start()
    own_ring.forward()
    q_ring.forward()

    proj_copy.wait()
    proj_ring = ring(lambda o, h: proj.at[o, h * 1024 : (h + 1) * 1024], at_x, x)
    proj_ring.start()

    k_swap.wait_recv()
    v_swap.wait_recv()
    mate_ring.start()
    q_ring.near()
    q_ring.far()

    skip_at = take(2)
    to_twin(skip_ref, skip, skip_at)
    to_twin(gain_ref, gain, skip_at + 1)

    def tile(s, c, zo, yo, masked):
        q = jnp.concatenate(
            [qbuf[s, c * 32 : (c + 1) * 32, j * 128 : (j + 1) * 128] for j in range(8)], axis=0
        )
        raw = lax.dot_general(
            q, kbuf[zo, yo], (((1,), (1,)), ((), ())), preferred_element_type=F32
        )
        if masked:
            base = 8 * zo + 2 * x + yo
            first = pl.multiple_of(base * 32, 32)
            loc = loc_col[pl.ds(first, 32), 0:1] - base * 1024
            loc = jnp.concatenate([loc] * 8, axis=0)
            pos = lax.broadcasted_iota(jnp.int32, raw.shape, 1)
            raw = jnp.where(pos <= loc, raw, LOW)
        top = jnp.max(raw, axis=1, keepdims=True)
        w = jnp.exp2((raw - top) * EXP2_SCALE)
        total = jnp.sum(w, axis=1, keepdims=True)
        part = jnp.dot(w.astype(BF16), vbuf[zo, yo], preferred_element_type=F32)
        m_old = m_s[s, c]
        m_new = jnp.maximum(m_old, top)
        a = jnp.exp2((m_old - m_new) * EXP2_SCALE)
        b = jnp.exp2((top - m_new) * EXP2_SCALE)
        m_s[s, c] = m_new
        l_s[s, c] = l_s[s, c] * a + total * b
        acc[s, c] = acc[s, c] * a + part * b

    def work(s, zo, yo):
        chunk = 8 * s + 2 * z
        block = 8 * zo + 2 * x + yo

        @pl.when(chunk > block)
        def _():
            tile(s, 0, zo, yo, False)
            tile(s, 1, zo, yo, False)

        @pl.when(chunk == block)
        def _():
            tile(s, 0, zo, yo, True)
            tile(s, 1, zo, yo, False)

        @pl.when(chunk + 1 == block)
        def _():
            tile(s, 1, zo, yo, True)

    part_at = take(8)

    def acc_copy(s):
        return remote(acc.at[s], racc.at[x], s_s.at[part_at + s], r_s.at[part_at + x], at_x(s))

    def stat_copy(s):
        return remote(part_stat.at[s], rstat.at[x], s_s.at[part_at + 4 + s],
                      r_s.at[part_at + 4 + x], at_x(s))

    @pl.loop(0, 8)
    def _(p):
        @pl.when(p == 2)
        def _():
            own_ring.up[1].wait_recv()

        @pl.when(p == 3)
        def _():
            own_ring.down[0].wait_recv()
            mate_ring.forward()

        @pl.when(p == 4)
        def _():
            mate_ring.up[1].wait_recv()
            proj_ring.forward()

        @pl.when(p == 5)
        def _():
            mate_ring.down[0].wait_recv()

        @pl.when(p == 6)
        def _():
            own_ring.far()

        @pl.when(p == 7)
        def _():
            mate_ring.far()

        step = jnp.where(p < 2, 0, jnp.where(p >= 6, 2, jnp.where(lax.rem(p, 2) == 0, 3, 1)))
        is_own = (p == 0) | (p == 2) | (p == 3) | (p == 6)
        zo = around(z, step)
        yo = jnp.where(is_own, yh, mate)

        @pl.loop(0, 4)
        def _(i):
            s = around(x, jnp.where(i == 0, 2, jnp.where(i == 1, 1, jnp.where(i == 2, 3, 0))))
            work(s, zo, yo)

            @pl.when(p == 7)
            def _():
                lane = lax.broadcasted_iota(jnp.int32, (32, 128), 1)
                for c in range(2):
                    t = jnp.zeros((32, 128), F32)
                    for j in range(8):
                        rows = slice(j * 32, (j + 1) * 32)
                        t = jnp.where(lane == j, m_s[s, c, rows, :], t)
                        t = jnp.where(lane == 8 + j, l_s[s, c, rows, :], t)
                    part_stat[s, c] = t

                @pl.when(s != x)
                def _():
                    acc_copy(s).start()
                    stat_copy(s).start()

                @pl.when(s == x)
                def _():
                    pltpu.make_async_copy(acc.at[s], racc.at[x], r_s.at[part_at + x]).start()
                    pltpu.make_async_copy(part_stat.at[s], rstat.at[x], r_s.at[part_at + 4 + x]).start()

    lex_copy.start()
    for i in range(4):
        remote(part_stat.at[i], rstat.at[i], s_s.at[part_at + 4 + i], r_s.at[part_at + 4 + i],
               at_x(around(x, 1))).wait_recv()
        remote(acc.at[i], racc.at[i], s_s.at[part_at + i], r_s.at[part_at + i],
               at_x(around(x, 1))).wait_recv()

    for c in range(2):
        tops = [rstat[i, c] for i in range(4)]
        sums = [pltpu.roll(t, 120, 1) for t in tops]
        top = jnp.maximum(jnp.maximum(tops[0], tops[1]), jnp.maximum(tops[2], tops[3]))
        shares = [jnp.exp2((t - top) * EXP2_SCALE) for t in tops]
        den = sum(a * b for a, b in zip(shares, sums))
        joined_rows = []
        for j in range(8):
            rows = slice(j * 32, (j + 1) * 32)
            num = sum(shares[i][:, j : j + 1] * racc[i, c, rows, :] for i in range(4))
            joined_rows.append((num / den[:, j : j + 1]).astype(BF16))
        rows_all[z, c * 32 : (c + 1) * 32, pl.ds(pl.multiple_of(yh * 1024, 1024), 1024)] = (
            jnp.concatenate(joined_rows, axis=1)
        )
    for i in range(4):
        @pl.when(i != x)
        def _():
            acc_copy(i).wait_send()
            stat_copy(i).wait_send()
    for i in range(2):
        @pl.when(jnp.logical_not(diagonal & (i == yh)))
        def _():
            q_send(i).wait_send()

    def rows_at(o, yo, h):
        return rows_all.at[o, :, pl.ds(pl.multiple_of(yo * 1024 + h * 512, 512), 512)]

    own_cols = pl.ds(pl.multiple_of(yh * 1024, 1024), 1024)
    pair = single(rows_all.at[z, :, own_cols], rows_all.at[z, :, own_cols], {"ctx_2": mate})
    pair.start()
    own_rows = ring(lambda o, h: rows_at(o, yh, h), at_z, z)
    mate_rows = ring(lambda o, h: rows_at(o, mate, h), at_z, z)
    own_rows.start()
    pair.wait_recv()
    mate_rows.start()
    own_rows.forward()
    mate_rows.forward()
    for r in (own_rows, mate_rows):
        r.near()
        r.far()
    proj_ring.near()
    proj_ring.far()

    def project(a, b):
        return jnp.dot(
            rows_all[...].reshape(256, 2048), proj[2 * a + b], preferred_element_type=F32
        )

    cross_at = take(2)
    away = 1 - yl
    mixed[away, other] = project(away, other)
    crossing_away = remote(
        mixed.at[away, other], from_core.at[away], s_s.at[cross_at], r_s.at[cross_at + away], at_core(other)
    )
    crossing_away.start()
    mixed[away, core] = project(away, core)
    mixed[yl, other] = project(yl, other)
    crossing_home = remote(
        mixed.at[yl, other], from_core.at[yl], s_s.at[cross_at + 1], r_s.at[cross_at + yl], at_core(other)
    )
    crossing_home.start()
    crossing_away.wait_recv()
    from_core[away] = mixed[away, core] + from_core[away]
    c = single(from_core.at[away], from_y, {"head_0": away})
    c.start()
    mixed[yl, core] = project(yl, core)
    crossing_home.wait_recv()
    from_core[yl] = mixed[yl, core] + from_core[yl]
    pending.append(crossing_away.wait_send)
    pending.append(crossing_home.wait_send)
    from_twin(skip_ref, skip, skip_at)
    from_twin(gain_ref, gain, skip_at + 1)
    c.wait_recv()
    hidden = (skip[...].astype(F32) + (from_core[yl] + from_y[...])).astype(BF16)
    back[0] = hidden
    back_at = take(1)
    to_twin(back.at[0], back.at[1], back_at)
    wide = hidden.astype(F32)

    part = jnp.sum(jnp.transpose(wide * wide), axis=0, keepdims=True)
    sq_c[core] = jnp.broadcast_to(part, (8, 256))
    c = single(sq_c.at[core], sq_c.at[core], at_core(other))
    c.start()
    c.wait_recv()
    sq[z, y] = sq_c[0] + sq_c[1]
    shared = []
    for d in range(4):
        for e in range(4):
            if d or e:
                peer = {**at_z(around(z, d)), **at_y(around(y, e))}
                c = single(sq.at[z, y], sq.at[z, y], peer)
                c.start()
                shared.append(c)
    for c in shared:
        c.wait_recv()
    part = sum(sq[i // 4, i % 4, 0:1] for i in range(16))
    factor = jnp.transpose(jnp.broadcast_to(lax.rsqrt(part / D + EPS), (256, 256)))
    norm[z, x, y, core] = (wide * factor * gain[...]).astype(BF16)

    r0, r1, r2 = pl.ds(0, 96), pl.ds(96, 80), pl.ds(176, 80)

    def cols(h):
        return pl.ds(h * 128, 128)

    own = norm.at[z, x, y, core]
    near = []
    for d in (2, 1, 3):
        for rows, dev, me in ((r0, at_z, z), (r1, at_x, x), (r2, at_y, y)):
            c = single(own.at[rows], own.at[rows], dev(around(me, d)))
            c.start()
            near.append(c)
    for c in near:
        c.wait_recv()
    run_rings([
        ring(lambda o, h: norm.at[:, o, y, core, r0, cols(h)], at_x, x),
        ring(lambda o, h: norm.at[z, :, o, core, r1, cols(h)], at_y, y),
        ring(lambda o, h: norm.at[o, x, :, core, r2, cols(h)], at_z, z),
    ])
    earlier = list(pending)
    pending.clear()
    last = [
        ring(lambda o, h: norm.at[:, :, o, core, r0, cols(h)], at_y, y),
        ring(lambda o, h: norm.at[o, :, :, core, r1, cols(h)], at_z, z),
        ring(lambda o, h: norm.at[:, o, :, core, r2, cols(h)], at_x, x),
    ]
    parts = [
        lambda o: norm.at[:, :, o, core, r0],
        lambda o: norm.at[o, :, :, core, r1],
        lambda o: norm.at[:, o, :, core, r2],
    ]
    arrivals = []

    def hand_over(ref):
        c = single(ref, ref, at_core(other))
        c.start()
        arrivals.append(c)

    for r in last:
        r.start()
    for f, own in zip(parts, (y, z, x)):
        hand_over(f(own))
    for r in last:
        r.forward()
    for wait in earlier:
        wait()
    twin_sent(skip_ref, skip, skip_at)
    twin_sent(gain_ref, gain, skip_at + 1)
    for r, f in zip(last, parts):
        r.near()
        hand_over(f(r.plus))
        hand_over(f(r.minus))
    for r, f in zip(last, parts):
        r.far()
        hand_over(f(r.opp))
    lex_copy.wait()

    def add(cc, fresh):
        for zz in range(4):
            first = zz * 2048 + cc * 512
            b = jnp.concatenate(
                [lex[pl.ds(pl.multiple_of(first + i * 1024, 512), 512), :] for i in range(2)], axis=0
            )
            for g in range(0, 4, GROUPS):
                a = jnp.concatenate([
                    jnp.concatenate([norm[zz, q, yy, cc] for yy in (0, 2, 1, 3)], axis=1)
                    for q in range(g, g + GROUPS)
                ], axis=0)
                t = jnp.dot(a, b, preferred_element_type=F32)
                rows = slice(g * 256, (g + GROUPS) * 256)
                if fresh and zz == 0:
                    logit[rows, :] = t
                else:
                    logit[rows, :] += t

    add(core, True)
    for c in arrivals:
        c.wait_recv()
    add(other, False)

    offset = (((z * 4 + x) * 2 + yh) * 4 + yl * 2 + core) * 512
    for group in range(4):
        rows = slice(group * 256, (group + 1) * 256)
        logits = logit[rows, :] / column(div_ref[:, rows])
        ids = lax.broadcasted_iota(jnp.int32, logits.shape, 1) + offset
        picked = jnp.sum(jnp.where(ids == column(tok_ref[:, rows]), logits, 0.0), axis=1, keepdims=True)
        peak = jnp.max(logits, axis=1, keepdims=True)
        total = jnp.sum(jnp.exp(logits - peak), axis=1, keepdims=True)
        lane = lax.broadcasted_iota(jnp.int32, (256, 128), 1)
        both = jnp.where(lane == 0, peak, jnp.where(lane == 1, total, picked))
        stat[0, z, :, rows] = jnp.transpose(both)[0:8, :]

    def joined(tiles):
        peak = tiles[0][0:1]
        for t in tiles[1:]:
            peak = jnp.maximum(peak, t[0:1])
        total = sum(t[1:2] * jnp.exp(t[0:1] - peak) for t in tiles)
        picked = sum(t[2:3] for t in tiles)
        return peak, total, picked

    def spread(values):
        sub = lax.broadcasted_iota(jnp.int32, (8, 1024), 0)
        return jnp.where(sub == 0, values[0], jnp.where(sub == 1, values[1], values[2]))

    values = None
    for stage, (dev, me) in enumerate(((at_z, z), (at_x, x), (at_y, y))):
        if stage:
            stat[stage, me] = spread(values)
        swap(stat.at[stage], dev, me)
        values = joined([stat[stage, i] for i in range(4)])
    stat_c[core] = spread(values)
    c = single(stat_c.at[core], stat_c.at[core], at_core(other))
    c.start()
    c.wait_recv()
    peak, total, picked = joined([stat_c[0], stat_c[1]])
    logprob_ref[...] = picked - peak - jnp.log(total)

    from_twin(back.at[0], back.at[1], back_at)
    hidden_ref[...] = back[1]
    twin_sent(back.at[0], back.at[1], back_at)
    for wait in pending:
        wait()


def whole(q, k, v, loc, proj, skip, gain, lex, div, tok):
    vmem = pl.BlockSpec(memory_space=pltpu.VMEM)
    hbm = pl.BlockSpec(memory_space=pl.ANY)
    return pl.pallas_call(
        kernel,
        out_shape=(
            jax.ShapeDtypeStruct((256, 256), BF16),
            jax.ShapeDtypeStruct((1, 1024), F32),
        ),
        in_specs=[hbm] * 10,
        out_specs=(vmem, vmem),
        scratch_shapes=[
            pltpu.VMEM((1, 1024), jnp.int32),
            pltpu.VMEM((1, 1024), F32),
            pltpu.VMEM((1, 1024), jnp.int32),
            pltpu.VMEM((4, 64, 1024), BF16),
            pltpu.VMEM((4, 2, 1024, 128), BF16),
            pltpu.VMEM((4, 2, 1024, 128), BF16),
            pltpu.VMEM((1024, 128), jnp.int32),
            pltpu.VMEM((4, 2, 256, 1), F32),
            pltpu.VMEM((4, 2, 256, 1), F32),
            pltpu.VMEM((4, 2, 256, 128), F32),
            pltpu.VMEM((4, 2, 32, 128), F32),
            pltpu.VMEM((4, 2, 256, 128), F32),
            pltpu.VMEM((4, 2, 32, 128), F32),
            pltpu.VMEM((4, 64, 2048), BF16),
            pltpu.VMEM((4, 2048, 256), BF16),
            pltpu.VMEM((2, 2, 256, 256), F32),
            pltpu.VMEM((2, 256, 256), F32),
            pltpu.VMEM((256, 256), F32),
            pltpu.VMEM((256, 256), BF16),
            pltpu.VMEM((1, 256), F32),
            pltpu.VMEM((2, 256, 256), BF16),
            pltpu.VMEM((2, 8, 256), F32),
            pltpu.VMEM((4, 4, 8, 256), F32),
            pltpu.VMEM((4, 4, 4, 2, 256, 256), BF16),
            pltpu.VMEM((8192, 512), BF16),
            pltpu.VMEM((1024, 512), F32),
            pltpu.VMEM((3, 4, 8, 1024), F32),
            pltpu.VMEM((2, 8, 1024), F32),
            pltpu.SemaphoreType.DMA((7,)),
            pltpu.SemaphoreType.DMA((192,)),
            pltpu.SemaphoreType.DMA((192,)),
        ],
        compiler_params=pltpu.CompilerParams(
            collective_id=0, has_side_effects=True, vmem_limit_bytes=58 * 1024 * 1024
        ),
        name="whole",
    )(q, k, v, loc, proj, skip, gain, lex, div, tok)


def shards(q, k, v, loc, proj, skip, gain, lex, div, tok):
    hidden, logprob = whole(
        q, k, v, loc.reshape(1, 1024), proj, skip, gain.reshape(1, 256), lex,
        div.reshape(1, 1024), tok.reshape(1, 1024)
    )
    return hidden, logprob.reshape(1024)


def solution(mesh):
    torus = Mesh(mesh.devices.reshape(4, 4, 2, 2, 2), CTX_HEAD)
    placed = (
        P(CTX, HEAD),
        P(CTX, HEAD),
        P(CTX, HEAD),
        P(),
        P(HEAD, CTX),
        P(HEAD, CTX),
        P(CTX),
        P(None, CTX_HEAD),
        P(),
        P(),
    )
    return jax.shard_map(
        shards, mesh=torus, in_specs=placed, out_specs=(P(HEAD, CTX), P()), check_vma=False
    )
```
